256 devices in a mesh: req: 16 (over z, core), wa: 16 (over x, y).
Axes of the slice: x: 4, y: 4, z: 8, core: 2. Of those that a mesh axis runs over, the one named last changes fastest.
Arguments:
- projected: bfloat16 [3, 2048, 2, 8192], P(None, 'req', None, 'wa'), may hold values from -6 to 6
- conv_weight: bfloat16 [4, 8192], P(None, 'wa'), may hold values from -3 to 3
- conv_bias: float32 [8192], P('wa'), may hold values from -3 to 3
- xproj_weight: bfloat16 [8192, 544], P('wa'), may hold values from -0.0625 to 0.0625
- dtproj_weight: bfloat16 [512, 8192], P(None, 'wa'), may hold values from -0.25 to 0.25
- dt_bias: float32 [8192], P('wa'), may hold values from -4 to -0.5
- a_rate: float32 [16, 8192], P(None, 'wa'), may hold values from 0.1 to 8
- skip_gain: float32 [8192], P('wa'), may hold values from 0.5 to 1.5
- ssm_state: float32 [2048, 16, 8192], P('req', None, 'wa'), may hold values from -6 to 6
- conv_cache: bfloat16 [2048, 3, 8192], P('req', None, 'wa'), may hold values from -6 to 6
- send_dest: int32 [2048], P('req'), may hold values from 0 to 15, as said below
- recv_source: int32 [2048], P('req'), may hold values from 0 to 15, as said below
- active: int32 [2048], P('req'), may hold values from 0 to 1, as said below
Outputs:
- gated_out: bfloat16 [3, 2048, 8192], P(None, 'req', 'wa')
- state_out: float32 [2048, 16, 8192], P('req', None, 'wa')
- cache_out: bfloat16 [2048, 3, 8192], P('req', None, 'wa')
The draws below stay inside these ranges and needn't reach their ends.
Inputs may be any that keep to these rules, and one draw needn't show every extreme that they name: `send_dest`: A slot whose request stays names its own device. From one device to one other device at most 2 requests move, and in every draw some device receives exactly 2 from every other device. No slot both leaves and receives. `recv_source`: A slot that receives nothing names its own device. The number of slots of device j naming device i equals the number of slots of i whose send_dest is j. `active`: every receiving slot is 1 and every slot left by a leaving request without a new one is 0.
All inputs are finite; a program needn't handle non-finite values.
Results may differ from the reference program's by a relative error of at most 0.0056.
Values sent between devices are 32-bit elements; how exact they have to be, the bound alone decides.
No kernel may reach another device: no remote copies, remote signals or barrier semaphores. Data moves between devices by JAX's collectives and lax.ppermute only.
A program may use at most 64 MiB of HBM per device.

```python
import math
import jax
import jax.numpy as jnp
from jax import lax

N = 16
KCONV = 4
DT_RANK = 512
DIW = 8192
STEPS = 3
CAP = 2
R_DEV = 128
REQS = 2048
N_REQ = 16


def shuffle_one(subkey):
    return jax.random.permutation(subkey, R_DEV).astype(jnp.int32)


def migration_plan(key):
    subkeys = jax.random.split(key, 6)
    heavy_source = jax.random.randint(subkeys[0], (N_REQ, 1), 0, 2)
    strong = jax.random.randint(subkeys[1], (N_REQ, N_REQ), 0, CAP + 1)
    weak_counts = jax.random.randint(subkeys[2], (N_REQ, N_REQ), 0, CAP // 2 + 1)
    counts = jnp.where(heavy_source == 1, strong, weak_counts)
    column = jax.random.randint(subkeys[3], (), 0, N_REQ)
    device_ids = jnp.arange(N_REQ, dtype=jnp.int32)
    counts = jnp.where(device_ids[None, :] == column, CAP, counts)
    counts = jnp.where(device_ids[:, None] == device_ids[None, :], 0, counts).astype(jnp.int32)
    leave_total = jnp.sum(counts, axis=1)
    come_total = jnp.sum(counts, axis=0)
    leave_edge = jnp.cumsum(counts, axis=1)
    come_edge = jnp.transpose(jnp.cumsum(counts, axis=0))
    positions = jnp.arange(R_DEV, dtype=jnp.int32)
    leaver = positions[None, :] < leave_total[:, None]
    destination = jnp.sum((leave_edge[:, None, :] <= positions[None, :, None]).astype(jnp.int32), axis=2)
    destination = jnp.where(leaver, destination, device_ids[:, None])
    shifted = positions[None, :] - leave_total[:, None]
    arrive = (shifted >= 0) & (shifted < come_total[:, None])
    source = jnp.sum((come_edge[:, None, :] <= shifted[:, :, None]).astype(jnp.int32), axis=2)
    source = jnp.where(arrive, source, device_ids[:, None])
    stay_alive = (jax.random.randint(subkeys[4], (N_REQ, R_DEV), 0, 8) > 0).astype(jnp.int32)
    alive = jnp.where(arrive, 1, jnp.where(leaver, 0, stay_alive))
    shuffles = jax.vmap(shuffle_one)(jax.random.split(subkeys[5], N_REQ))
    destination = jnp.take_along_axis(destination, shuffles, axis=1)
    source = jnp.take_along_axis(source, shuffles, axis=1)
    alive = jnp.take_along_axis(alive, shuffles, axis=1)
    return (destination.reshape(-1).astype(jnp.int32), source.reshape(-1).astype(jnp.int32), alive.reshape(-1).astype(jnp.int32))


def draw_send_dest(key, part):
    return migration_plan(key)[0]


def draw_recv_source(key, part):
    return migration_plan(key)[1]


def draw_active(key, part):
    return migration_plan(key)[2]


def levels(own_key, shape, cuts, low, high):
    level = 1.0
    for position, parts in cuts:
        heights = jax.random.uniform(jax.random.fold_in(jax.random.fold_in(own_key, 6), position), (parts,), jnp.float32, low / len(cuts), high / len(cuts))
        level = level * jnp.repeat(jnp.exp(heights), shape[position] // parts).reshape((-1,) + (1,) * (len(shape) - 1 - position))
    return level


def noise(stream_key, shape, deviation, reach, pieces=(), kind=jnp.bfloat16):
    level = levels(stream_key, shape, pieces, -0.22, 0.18) if pieces else 1.0
    array = jax.random.normal(stream_key, shape, jnp.float32) * deviation * level
    return jnp.minimum(jnp.maximum(array, -reach), reach).astype(kind)


def setup_inputs(seed: int = 0) -> dict:
    key_list = jax.random.split(jax.random.key(seed), 14)
    projected = noise(key_list[0], (STEPS, REQS, 2, DIW), 1.0, 6.0, ((1, 16), (3, 16)))
    conv_weight = noise(key_list[1], (KCONV, DIW), 0.5, 3.0, ((1, 16),))
    conv_bias = noise(key_list[2], (DIW,), 0.5, 3.0, ((0, 16),), jnp.float32)
    xproj_weight = noise(key_list[3], (DIW, DT_RANK + 2 * N), DIW ** -0.5, 0.0625, ((0, 16),))
    dtproj_weight = noise(key_list[4], (DT_RANK, DIW), DT_RANK ** -0.5, 0.25, ((1, 16),))
    dt_bias = jnp.clip(-4.0 + 3.5 * jax.random.uniform(key_list[5], (DIW,), jnp.float32) ** levels(key_list[5], (DIW,), ((0, 16),), -0.2, 0.2), -4.0, -0.5)
    a_rate = jnp.clip(jnp.exp(math.log(8.0) - 4.3820266 * jax.random.uniform(key_list[6], (N, DIW), jnp.float32) ** levels(key_list[6], (N, DIW), ((1, 16),), -0.2, 0.2)), 0.1, 8.0)
    skip_gain = jnp.clip(0.5 + 1.0 * jax.random.uniform(key_list[7], (DIW,), jnp.float32) ** levels(key_list[7], (DIW,), ((0, 16),), -0.2, 0.2), 0.5, 1.5)
    ssm_state = noise(key_list[8], (REQS, N, DIW), 1.0, 6.0, ((0, 16), (2, 16)), jnp.float32)
    conv_cache = noise(key_list[9], (REQS, KCONV - 1, DIW), 1.0, 6.0, ((0, 16), (2, 16)))
    send_dest = draw_send_dest(jax.random.fold_in(key_list[13], 71), 0)
    recv_source = draw_recv_source(jax.random.fold_in(key_list[13], 71), 0)
    active = draw_active(jax.random.fold_in(key_list[13], 71), 0)
    return {"projected": projected, "conv_weight": conv_weight, "conv_bias": conv_bias, "xproj_weight": xproj_weight, "dtproj_weight": dtproj_weight, "dt_bias": dt_bias, "a_rate": a_rate, "skip_gain": skip_gain, "ssm_state": ssm_state, "conv_cache": conv_cache, "send_dest": send_dest, "recv_source": recv_source, "active": active}


def slot_ranks(targets):
    onehot = (targets[:, None] == jnp.arange(N_REQ, dtype=jnp.int32)[None, :]).astype(jnp.int32)
    onehot = onehot.reshape(N_REQ, R_DEV, N_REQ)
    earlier = jnp.cumsum(onehot, axis=1) - onehot
    return jnp.sum(earlier * onehot, axis=2).reshape(-1).astype(jnp.int32)


def migrate(ssm_state, conv_cache, send_dest, recv_source):
    owners = (jnp.arange(REQS, dtype=jnp.int32) // R_DEV).astype(jnp.int32)
    send_rank = jnp.minimum(slot_ranks(send_dest), CAP - 1)
    recv_rank = jnp.minimum(slot_ranks(recv_source), CAP - 1)
    leaving = send_dest != owners
    arriving = recv_source != owners
    bucket_key = (owners * N_REQ + send_dest) * CAP + send_rank
    bucket_key = jnp.where(leaving, bucket_key, N_REQ * N_REQ * CAP).astype(jnp.int32)
    anchor_table = jnp.zeros((N_REQ * N_REQ * CAP + 1,), jnp.int32).at[bucket_key].set(jnp.arange(REQS, dtype=jnp.int32))
    wanted = ((recv_source * N_REQ + owners) * CAP + recv_rank).astype(jnp.int32)
    anchor = anchor_table[wanted]
    arriving_b = arriving[:, None, None]
    leaving_b = leaving[:, None, None]
    moved_state = jnp.where(arriving_b, ssm_state[anchor], jnp.where(leaving_b, jnp.float32(0.0), ssm_state))
    moved_cache = jnp.where(arriving_b, conv_cache[anchor], jnp.where(leaving_b, jnp.zeros_like(conv_cache), conv_cache))
    return moved_state, moved_cache


def reference(projected, conv_weight, conv_bias, xproj_weight, dtproj_weight, dt_bias, a_rate, skip_gain, ssm_state, conv_cache, send_dest, recv_source, active):
    moved_state, moved_cache = migrate(ssm_state, conv_cache, send_dest, recv_source)
    x_part = projected[:, :, 0]
    z_part = projected[:, :, 1]
    window = jnp.concatenate([jnp.transpose(moved_cache, (1, 0, 2)), x_part], axis=0)
    conv_taps = conv_weight.astype(jnp.float32)
    conv_list = []
    for step_index in range(STEPS):
        total = conv_bias[None, :]
        for tap_index in range(KCONV):
            total = total + conv_taps[tap_index][None, :] * window[step_index + tap_index].astype(jnp.float32)
        conv_list.append(jax.nn.silu(total).astype(jnp.bfloat16))
    conv_out = jnp.stack(conv_list)
    mixed = jnp.dot(conv_out.reshape(STEPS * REQS, DIW), xproj_weight, preferred_element_type=jnp.float32)
    rank_part = mixed[:, :DT_RANK].astype(jnp.bfloat16)
    step_size = jax.nn.softplus(jnp.dot(rank_part, dtproj_weight, preferred_element_type=jnp.float32) + dt_bias[None, :])
    mixed = mixed.reshape(STEPS, N_REQ, R_DEV, DT_RANK + 2 * N)
    step_size = step_size.reshape(STEPS, N_REQ, R_DEV, DIW)
    conv_blocks = conv_out.reshape(STEPS, N_REQ, R_DEV, DIW)
    gate_blocks = z_part.reshape(STEPS, N_REQ, R_DEV, DIW)
    alive_blocks = (active == 1).reshape(N_REQ, R_DEV)
    state_blocks = moved_state.reshape(N_REQ, R_DEV, N, DIW)

    def decode_block(inputs):
        state, conv_block, mixed_block, step_block, gate_block, alive = inputs
        alive_b = alive[:, None, None]
        results = []
        for step_index in range(STEPS):
            conv_value = conv_block[step_index].astype(jnp.float32)
            b_part = mixed_block[step_index][:, DT_RANK:DT_RANK + N]
            c_part = mixed_block[step_index][:, DT_RANK + N:]
            step_now = step_block[step_index]
            decay = jnp.exp(-step_now[:, None, :] * a_rate[None, :, :])
            updated = decay * state + (step_now * conv_value)[:, None, :] * b_part[:, :, None]
            state = jnp.where(alive_b, updated, state)
            readout = jnp.sum(c_part[:, :, None] * state, axis=1) + skip_gain[None, :] * conv_value
            gated = readout * jax.nn.silu(gate_block[step_index].astype(jnp.float32))
            results.append(jnp.where(alive[:, None], gated, jnp.float32(0.0)).astype(jnp.bfloat16))
        return jnp.stack(results), state

    moved_axes = (state_blocks, jnp.transpose(conv_blocks, (1, 0, 2, 3)), jnp.transpose(mixed, (1, 0, 2, 3)),
                  jnp.transpose(step_size, (1, 0, 2, 3)), jnp.transpose(gate_blocks, (1, 0, 2, 3)), alive_blocks)
    gated_blocks, final_blocks = lax.map(decode_block, moved_axes)
    gated_out = jnp.transpose(gated_blocks, (1, 0, 2, 3)).reshape(STEPS, REQS, DIW)
    state_out = final_blocks.reshape(REQS, N, DIW)
    new_cache = jnp.transpose(window[STEPS:], (1, 0, 2))
    cache_out = jnp.where((active == 1)[:, None, None], new_cache, moved_cache)
    return gated_out, state_out, cache_out
```

```python
import math

import jax
import jax.numpy as jnp
from jax import lax
from jax.experimental import pallas as pl
from jax.experimental.pallas import tpu as pltpu
from jax.sharding import PartitionSpec as P

CAP = 2
SIDE = 4
MIB = 1 << 20
F32 = jnp.float32
BF16 = jnp.bfloat16
VM = pl.BlockSpec(memory_space=pltpu.VMEM)
SM = pl.BlockSpec(memory_space=pltpu.SMEM)
HB = pl.BlockSpec(memory_space=pl.ANY)


def shift(axis, amount):
    pairs = []
    for x in range(SIDE):
        for y in range(SIDE):
            tx, ty = (x + amount) % SIDE, y
            if axis == 1:
                tx, ty = x, (y + amount) % SIDE
            pairs.append((x * SIDE + y, tx * SIDE + ty))
    return pairs


def dot_t(lhs, rhs):
    return lax.dot_general(lhs, rhs, (((1,), (1,)), ((), ())), preferred_element_type=F32)


def dot_n(lhs, rhs):
    return jnp.dot(lhs, rhs, preferred_element_type=F32)


def iota(shape, dim):
    return lax.broadcasted_iota(jnp.int32, shape, dim)


def as_column(row, size):
    eye = iota((size, size), 0) == iota((size, size), 1)
    return jnp.sum(jnp.where(eye, jnp.broadcast_to(row, (size, size)), 0), axis=1, keepdims=True)


def ranks_row(row, col, size):
    earlier = (col == row) & (iota((size, size), 0) < iota((size, size), 1))
    return jnp.sum(jnp.where(earlier, 1, 0), axis=0, keepdims=True)


def ranks_col(row, col, size):
    earlier = (col == row) & (iota((size, size), 1) < iota((size, size), 0))
    return jnp.sum(jnp.where(earlier, 1, 0), axis=1, keepdims=True)


def pick_cache_kernel(pos_ref, dest_ref, cache_ref, out_ref):
    taps, slots, _ = cache_ref.shape
    own = pos_ref[0]
    row = dest_ref[...]
    rank = ranks_row(row, as_column(row, slots), slots)
    rows = out_ref.shape[0]
    shape = (rows, slots)
    target = iota(shape, 0) // 8
    place = iota(shape, 0) % 8
    total = jnp.zeros(out_ref.shape, F32)
    hit = (row == target) & (row != own) & (rank == place % CAP)
    for tap in range(taps):
        pick = jnp.where(hit & (place // CAP == tap), 1.0, 0.0).astype(BF16)
        total = total + dot_n(pick, cache_ref[tap])
    out_ref[...] = total


def pick_state_kernel(pos_ref, dest_ref, source_ref, state_ref, out_ref, from_ref, pick, count, sems):
    slots = state_ref.shape[0]
    buckets = out_ref.shape[0]
    own = pos_ref[0]

    def clear(i, carry):
        pick[i] = 0
        count[i] = 0
        return carry

    lax.fori_loop(0, buckets, clear, 0)
    peers = buckets // CAP

    def plan(s, carry):
        target = dest_ref[s]
        leaving = target != own
        source = source_ref[s]
        arriving = source != own
        from_ref[s] = jnp.where(leaving, -2, -1)

        @pl.when(leaving)
        def _():
            rank = count[target]
            pick[target * CAP + jnp.minimum(rank, CAP - 1)] = s
            count[target] = rank + 1

        @pl.when(arriving)
        def _():
            rank = count[peers + source]
            from_ref[s] = source * CAP + jnp.minimum(rank, CAP - 1)
            count[peers + source] = rank + 1

        return carry

    lax.fori_loop(0, slots, plan, 0)
    for b in range(buckets):
        pltpu.make_async_copy(state_ref.at[pick[b]], out_ref.at[b], sems.at[b]).start()
    for b in range(buckets):
        pltpu.make_async_copy(state_ref.at[pick[b]], out_ref.at[b], sems.at[b]).wait()


def conv_steps(window, taps_ref, bias, steps):
    taps = taps_ref[...].astype(F32)
    outs = []
    for t in range(steps):
        total = bias
        for k in range(taps.shape[0]):
            total = total + taps[k : k + 1, :] * window[t + k]
        outs.append(jax.nn.silu(total).astype(BF16))
    return outs


def main_kernel(pos_ref, dest_ref, active_ref, x_ref, cache_ref, taps_ref, bias_ref, proj_ref,
                conv_ref, cache_out_ref, a0, a1, a2, a3, b0, b1, b2, b3, mix, low):
    steps, slots, width = x_ref.shape
    taps = cache_ref.shape[0]
    rank_width = width
    own = pos_ref[0]
    dest = as_column(dest_ref[...], slots)
    alive = as_column(active_ref[...], slots)
    step = 16
    for r in range(0, slots, step):
        rows = slice(r, r + step)
        keep = [cache_ref[j, rows, :] for j in range(taps)]
        new = [x_ref[t, rows, :] for t in range(steps)]
        outs = conv_steps([v.astype(F32) for v in keep + new], taps_ref, bias_ref[...], steps)
        for t in range(steps):
            conv_ref[t, rows, :] = outs[t]
        on = alive[rows, :] == 1
        gone = dest[rows, :] != own
        for j in range(taps):
            old = jnp.where(gone, 0.0, keep[j].astype(F32))
            cache_out_ref[j, rows, :] = jnp.where(on, new[j].astype(F32), old).astype(BF16)
    lhs = conv_ref[...].reshape(steps * slots, width)
    mix[...] = dot_t(lhs, proj_ref[0:rank_width, :])
    rest = proj_ref.shape[0] - rank_width
    low[:, 0:rest] = dot_t(lhs, proj_ref[rank_width:, :])
    quarter = slots // 2 // SIDE
    for half, outs in ((0, (a0, a1, a2, a3)), (1, (b0, b1, b2, b3))):
        for d in range(SIDE):
            q = lax.rem(pos_ref[1 + half] + d, SIDE)
            out = outs[d]
            out[steps * quarter :, :] = jnp.zeros((8, width), F32)
            for t in range(steps):
                start = pl.multiple_of(t * slots + half * (slots // 2) + q * quarter, quarter)
                out[t * quarter : (t + 1) * quarter, :] = mix[pl.ds(start, quarter), :]
                for g in range(quarter // 8):
                    lane = 32 * (t * (quarter // 8) + g)
                    out[steps * quarter :, lane : lane + rest] = low[pl.ds(start + 8 * g, 8), 0:rest]


def merge_kernel(pos_ref, source_ref, got_ref, x_ref, taps_ref, bias_ref, proj_ref,
                 a0, a1, a2, a3, b0, b1, b2, b3, conv_ref, to_x, to_y):
    steps, slots, width = x_ref.shape
    own = pos_ref[0]
    row = source_ref[...]
    rank = ranks_row(row, as_column(row, slots), slots)
    peers = got_ref.shape[0] // 8
    buckets = peers * CAP
    shape = (buckets, slots)
    peer, order = iota(shape, 0) % peers, iota(shape, 0) // peers
    hit = (row == peer) & (row != own) & (rank == order)
    pick = jnp.where(hit, 1.0, 0.0).astype(BF16)
    got = got_ref[...].astype(BF16)
    shape = (buckets, got.shape[0])
    peer, order = iota(shape, 0) % peers, iota(shape, 0) // peers
    window = []
    for j in range(taps_ref.shape[0] - 1):
        place = peer * 8 + j * CAP + order
        window.append(dot_n(jnp.where(iota(shape, 1) == place, 1.0, 0.0).astype(BF16), got))
    for t in range(steps):
        window.append(dot_n(pick, x_ref[t]))
    outs = conv_steps(window, taps_ref, bias_ref[...], steps)
    for t in range(steps):
        conv_ref[t * buckets : (t + 1) * buckets, :] = outs[t]
    lhs = conv_ref[...]
    mix = dot_t(lhs, proj_ref[0:width, :])
    low = dot_t(lhs, proj_ref[width:, :])
    rest = low.shape[1]
    half = steps * peers
    for part, out, pieces in ((0, to_x, (b0, b1, b2, b3)), (1, to_y, (a0, a1, a2, a3))):
        total = pieces[0][...] + pieces[1][...] + pieces[2][...] + pieces[3][...]
        out[0:half, :] = total[0:half, :]
        out[2 * half :, :] = total[half:, :]
        for t in range(steps):
            start = t * buckets + part * peers
            out[half + t * peers : half + (t + 1) * peers, :] = mix[start : start + peers, :]
            for g in range(peers // 8):
                lane = 32 * ((steps + t) * (peers // 8) + g)
                out[2 * half :, lane : lane + rest] = low[start + 8 * g : start + 8 * g + 8, :]


def scan_kernel(pos_ref, from_ref, source_ref, active_ref, x0, x1, x2, x3, y0, y1, y2, y3,
                conv_ref, conv_arr_ref, z_ref, dtw_ref, dtb_ref, rate_ref, gain_ref, state_ref, got_ref,
                gated_ref, out_ref, rank_s, low_s, step_s, conv_s, alive_s, rate_s, arr_s, state_s, in_sems, out_sems):
    steps, slots, width = conv_ref.shape
    states = rate_ref.shape[0]
    block = slots // in_sems.shape[0]

    def prepare():
        rate_s[...] = rate_ref[...] * (-1.0 / math.log(2.0))
        quarter = slots // 2 // SIDE
        half = steps * quarter
        groups = quarter // 8
        peers = got_ref.shape[0] // states // CAP
        buckets = peers * CAP
        rest = 2 * states
        for axis, pieces in ((0, (x0, x1, x2, x3)), (1, (y0, y1, y2, y3))):
            for d in range(SIDE):
                q = lax.rem(pos_ref[1 + axis] + (SIDE - d), SIDE)
                for t in range(steps):
                    start = pl.multiple_of(t * slots + axis * (slots // 2) + q * quarter, quarter)
                    rank_s[pl.ds(start, quarter), :] = pieces[d][t * quarter : (t + 1) * quarter, :].astype(BF16)
                    for g in range(groups):
                        lane = 32 * (t * groups + g)
                        low_s[pl.ds(start + 8 * g, 8), 0:rest] = pieces[d][2 * half :, lane : lane + rest]
        row = source_ref[...]
        col = as_column(row, slots)
        rank = ranks_col(row, col, slots)
        alive = as_column(active_ref[...], slots) == 1
        alive_s[...] = jnp.broadcast_to(jnp.where(alive, 1.0, 0.0), alive_s.shape)
        arriving = col != pos_ref[0]
        shape = (slots, buckets)
        hit = arriving & (col == iota(shape, 1) % peers) & (rank == iota(shape, 1) // peers)
        pick = jnp.where(hit, 1.0, 0.0)
        pick_low = pick.astype(BF16)
        total_x = x0[half:, :] + x1[half:, :] + x2[half:, :] + x3[half:, :]
        total_y = y0[half:, :] + y1[half:, :] + y2[half:, :] + y3[half:, :]
        for t in range(steps):
            rows = slice(t * slots, (t + 1) * slots)
            part = slice(t * peers, (t + 1) * peers)
            arr = jnp.concatenate([total_y[part, :], total_x[part, :]], axis=0).astype(BF16)
            rank_s[rows, :] = jnp.where(arriving, dot_n(pick_low, arr), rank_s[rows, :].astype(F32)).astype(BF16)
            for g in range(peers // 8):
                lane = 32 * ((steps + t) * (peers // 8) + g)
                arr_s[8 * g : 8 * g + 8, 0:rest] = total_y[half:, lane : lane + rest]
                arr_s[peers + 8 * g : peers + 8 * g + 8, 0:rest] = total_x[half:, lane : lane + rest]
            low_arr = jnp.dot(pick, arr_s[:, 0:rest], precision=lax.Precision.HIGHEST, preferred_element_type=F32)
            low_s[rows, 0:rest] = jnp.where(arriving, low_arr, low_s[rows, 0:rest])
            conv_arr = dot_n(pick_low, conv_arr_ref[t * buckets : (t + 1) * buckets, :])
            conv_s[rows, :] = jnp.where(arriving, conv_arr, conv_ref[t].astype(F32))
            raw = dot_n(rank_s[rows, :], dtw_ref[...]) + dtb_ref[...]
            soft = jnp.maximum(raw, 0.0) + jnp.log1p(jnp.exp(-jnp.abs(raw)))
            step_s[rows, :] = jnp.where(alive, soft, 0.0)

    tiles = width // 128

    def load(i, l):
        rows = pl.ds(i * block * states, block * states)
        return pltpu.make_async_copy(state_ref.at[rows, pl.ds(l * 128, 128)], state_s.at[l, rows], in_sems.at[i, l])

    def store(i, l):
        rows = pl.ds(i * block * states, block * states)
        return pltpu.make_async_copy(state_s.at[l, rows], out_ref.at[rows, pl.ds(l * 128, 128)], out_sems.at[i, l])

    for i in range(slots // block):
        for l in range(tiles):
            load(i, l).start()
    prepare()

    def group(base):
        for i in range(8):
            source = from_ref[base + i]
            here = pl.ds(pl.multiple_of((base + i) * states, states), states)

            @pl.when(source == -2)
            def _():
                for l in range(tiles):
                    state_s[l, here, :] = jnp.zeros((states, 128), F32)

            @pl.when(source >= 0)
            def _():
                there = pl.ds(pl.multiple_of(source * states, states), states)
                for l in range(tiles):
                    state_s[l, here, :] = got_ref[there, l * 128 : (l + 1) * 128]

        dts, dxs, lows, accs = [], [], [], []
        for t in range(steps):
            rows = pl.ds(pl.multiple_of(t * slots + base, 8), 8)
            lows.append(low_s[rows, :])
            for l in range(tiles):
                lanes = slice(l * 128, (l + 1) * 128)
                dt = step_s[rows, lanes]
                cv = conv_s[rows, lanes]
                dts.append(dt)
                dxs.append(dt * cv)
                accs.append(gain_ref[:, lanes] * cv)
        for n in range(states):
            place = pl.ds(base * states + n, 8, stride=states)
            gives = [jnp.broadcast_to(low[:, n : n + 1], (8, 128)) for low in lows]
            takes = [jnp.broadcast_to(low[:, states + n : states + n + 1], (8, 128)) for low in lows]
            for l in range(tiles):
                st = state_s[l, place, :]
                rate = rate_s[n : n + 1, l * 128 : (l + 1) * 128]
                for t in range(steps):
                    k = t * tiles + l
                    st = jnp.exp2(dts[k] * rate) * st + dxs[k] * gives[t]
                    accs[k] = accs[k] + st * takes[t]
                state_s[l, place, :] = st
        return accs

    def pair(i, carry):
        base = pl.multiple_of(i * 16, 16)
        accs = [group(base), group(pl.multiple_of(base + 8, 8))]
        on = alive_s[pl.ds(base, 16), :] > 0.5
        for t in range(steps):
            for l in range(tiles):
                lanes = slice(l * 128, (l + 1) * 128)
                gate = jax.nn.silu(z_ref[t, pl.ds(base, 16), lanes].astype(F32))
                value = jnp.concatenate([accs[0][t * tiles + l], accs[1][t * tiles + l]], axis=0) * gate
                gated_ref[t, pl.ds(base, 16), lanes] = jnp.where(on, value, 0.0).astype(BF16)
        return carry

    def chunk(i, carry):
        for l in range(tiles):
            load(i, l).wait()
        lax.fori_loop(i * (block // 16), (i + 1) * (block // 16), pair, 0)
        for l in range(tiles):
            store(i, l).start()
        return carry

    lax.fori_loop(0, slots // block, chunk, 0)
    for i in range(slots // block):
        for l in range(tiles):
            store(i, l).wait()


def on_device(projected, conv_weight, conv_bias, xproj_weight, dtproj_weight, dt_bias, a_rate, skip_gain,
              ssm_state, conv_cache, send_dest, recv_source, active):
    steps, slots, _, width = projected.shape
    rank_width = dtproj_weight.shape[0]
    states = a_rate.shape[0]
    taps = conv_weight.shape[0]
    peers = lax.axis_size("req")
    buckets = peers * CAP
    place = lax.axis_index("wa")
    pos = jnp.stack([lax.axis_index("req"), place // SIDE, place % SIDE]).astype(jnp.int32)
    send_row, recv_row, active_row = (v.reshape(1, slots) for v in (send_dest, recv_source, active))
    bias, dt_row, gain = (v.reshape(1, width) for v in (conv_bias, dt_bias, skip_gain))
    cache = jnp.transpose(conv_cache, (1, 0, 2))
    proj = jnp.transpose(xproj_weight, (1, 0))
    x_part = projected[:, :, 0]
    z_part = projected[:, :, 1]
    sds = jax.ShapeDtypeStruct

    out_cache = pl.pallas_call(
        pick_cache_kernel,
        out_shape=sds((peers * 8, width), F32),
        in_specs=[SM, VM, VM],
        out_specs=VM,
        compiler_params=pltpu.CompilerParams(vmem_limit_bytes=12 * MIB),
        name="pick_cache",
    )(pos, send_row, cache)
    got_cache = lax.all_to_all(
        out_cache.reshape(peers, 8, width), "req", split_axis=0, concat_axis=0, tiled=True
    ).reshape(peers * 8, width)

    out_state, came_from = pl.pallas_call(
        pick_state_kernel,
        out_shape=(sds((buckets, states, width), F32), sds((slots,), jnp.int32)),
        in_specs=[SM, SM, SM, HB],
        out_specs=(HB, SM),
        scratch_shapes=[
            pltpu.SMEM((buckets,), jnp.int32),
            pltpu.SMEM((buckets,), jnp.int32),
            pltpu.SemaphoreType.DMA((buckets,)),
        ],
        compiler_params=pltpu.CompilerParams(vmem_limit_bytes=4 * MIB),
        name="pick_state",
    )(pos, send_dest, recv_source, ssm_state)
    got_state = lax.all_to_all(out_state, "req", split_axis=0, concat_axis=0, tiled=True)

    half = steps * (slots // 2 // SIDE)
    main = pl.pallas_call(
        main_kernel,
        out_shape=(
            sds((steps, slots, width), BF16),
            sds((taps - 1, slots, width), BF16),
        )
        + (sds((half + 8, width), F32),) * (2 * SIDE),
        in_specs=[SM] + [VM] * 7,
        out_specs=(VM,) * (2 + 2 * SIDE),
        scratch_shapes=[pltpu.VMEM((steps * slots, width), F32), pltpu.VMEM((steps * slots, 128), F32)],
        compiler_params=pltpu.CompilerParams(vmem_limit_bytes=24 * MIB),
        name="conv_project",
    )(pos, send_row, active_row, x_part, cache, conv_weight, bias, proj)
    conv_main, cache_out = main[0], main[1]
    own_a, own_b = main[2 : 2 + SIDE], main[2 + SIDE :]
    piece_a = [own_a[0]] + [lax.ppermute(own_a[d], "wa", shift(0, d)) for d in range(1, SIDE)]
    piece_b = [own_b[0]] + [lax.ppermute(own_b[d], "wa", shift(1, d)) for d in range(1, SIDE)]

    conv_arr, to_x, to_y = pl.pallas_call(
        merge_kernel,
        out_shape=(
            sds((steps * buckets, width), BF16),
            sds((2 * half + 8, width), F32),
            sds((2 * half + 8, width), F32),
        ),
        in_specs=[SM] + [VM] * 14,
        out_specs=(VM,) * 3,
        compiler_params=pltpu.CompilerParams(vmem_limit_bytes=16 * MIB),
        name="merge_arrivals",
    )(pos, recv_row, got_cache, x_part, conv_weight, bias, proj, *piece_a, *piece_b)

    def summed(value, axis):
        others = [lax.ppermute(value, "wa", shift(axis, d)) for d in range(1, SIDE)]
        return value + others[0] + others[1] + others[2]

    from_y = summed(to_y, 1)
    from_x = summed(to_x, 0)
    last_x = [from_y] + [lax.ppermute(from_y, "wa", shift(0, d)) for d in range(1, SIDE)]
    last_y = [from_x] + [lax.ppermute(from_x, "wa", shift(1, d)) for d in range(1, SIDE)]

    gated_out, state_out = pl.pallas_call(
        scan_kernel,
        out_shape=(sds((steps, slots, width), BF16), sds((slots * states, width), F32)),
        in_specs=[SM, SM] + [VM] * 17 + [HB, VM],
        out_specs=(VM, HB),
        scratch_shapes=[
            pltpu.VMEM((steps * slots, width), BF16),
            pltpu.VMEM((steps * slots, 128), F32),
            pltpu.VMEM((steps * slots, width), F32),
            pltpu.VMEM((steps * slots, width), F32),
            pltpu.VMEM((slots, 128), F32),
            pltpu.VMEM((states, width), F32),
            pltpu.VMEM((buckets, 128), F32),
            pltpu.VMEM((width // 128, slots * states, 128), F32),
            pltpu.SemaphoreType.DMA((4, width // 128)),
            pltpu.SemaphoreType.DMA((4, width // 128)),
        ],
        compiler_params=pltpu.CompilerParams(vmem_limit_bytes=24 * MIB),
        name="scan",
    )(
        pos, came_from, recv_row, active_row, *last_x, *last_y, conv_main, conv_arr, z_part,
        dtproj_weight, dt_row, a_rate, gain, ssm_state.reshape(slots * states, width),
        got_state.reshape(buckets * states, width),
    )
    return (
        gated_out,
        state_out.reshape(slots, states, width),
        jnp.transpose(cache_out, (1, 0, 2)),
    )


def solution(mesh):
    return jax.shard_map(
        on_device,
        mesh=mesh,
        in_specs=(
            P(None, "req", None, "wa"),
            P(None, "wa"),
            P("wa"),
            P("wa", None),
            P(None, "wa"),
            P("wa"),
            P(None, "wa"),
            P("wa"),
            P("req", None, "wa"),
            P("req", None, "wa"),
            P("req"),
            P("req"),
            P("req"),
        ),
        out_specs=(P(None, "req", "wa"), P("req", None, "wa"), P("req", None, "wa")),
        check_vma=False,
    )
```

```python
import math

import jax
import jax.numpy as jnp
from jax import lax
from jax.experimental import pallas as pl
from jax.experimental.pallas import tpu as pltpu
from jax.sharding import PartitionSpec as P

CAP = 2
SIDE = 4
MIB = 1 << 20
F32 = jnp.float32
BF16 = jnp.bfloat16
VM = pl.BlockSpec(memory_space=pltpu.VMEM)
SM = pl.BlockSpec(memory_space=pltpu.SMEM)
HB = pl.BlockSpec(memory_space=pltpu.HBM)


def shift(axis, amount):
    pairs = []
    for x in range(SIDE):
        for y in range(SIDE):
            tx, ty = (x + amount) % SIDE, y
            if axis == 1:
                tx, ty = x, (y + amount) % SIDE
            pairs.append((x * SIDE + y, tx * SIDE + ty))
    return pairs


def dot_t(lhs, rhs):
    return lax.dot_general(lhs, rhs, (((1,), (1,)), ((), ())), preferred_element_type=F32)


def dot_n(lhs, rhs):
    return jnp.dot(lhs, rhs, preferred_element_type=F32)


def iota(shape, dim):
    return lax.broadcasted_iota(jnp.int32, shape, dim)


def as_column(row, size):
    eye = iota((size, size), 0) == iota((size, size), 1)
    return jnp.sum(jnp.where(eye, jnp.broadcast_to(row, (size, size)), 0), axis=1, keepdims=True)


def ranks_row(row, col, size):
    earlier = (col == row) & (iota((size, size), 0) < iota((size, size), 1))
    return jnp.sum(jnp.where(earlier, 1, 0), axis=0, keepdims=True)


def ranks_col(row, col, size):
    earlier = (col == row) & (iota((size, size), 1) < iota((size, size), 0))
    return jnp.sum(jnp.where(earlier, 1, 0), axis=1, keepdims=True)


def fetch(pairs, sems):
    copies = [pltpu.make_async_copy(a, b, sems.at[i]) for i, (a, b) in enumerate(pairs)]
    for copy in copies:
        copy.start()
    return copies


def pick_cache_kernel(pos_ref, dest_hbm, source_hbm, cache_hbm, out_ref, plan_ref, dest_ref, source_ref, cache_ref, sems):
    copies = fetch(((dest_hbm, dest_ref), (source_hbm, source_ref), (cache_hbm, cache_ref)), sems)
    for copy in copies[:2]:
        copy.wait()
    taps, slots, _ = cache_ref.shape
    own = pos_ref[0]
    row = dest_ref[...]
    col = as_column(row, slots)
    rank = ranks_row(row, col, slots)
    rows = out_ref.shape[0]
    shape = (rows, slots)
    target = iota(shape, 0) // 8
    place = iota(shape, 0) % 8
    total = jnp.zeros(out_ref.shape, F32)
    copies[2].wait()
    hit = (row == target) & (row != own) & (rank == place % CAP)
    for tap in range(taps):
        pick = jnp.where(hit & (place // CAP == tap), 1.0, 0.0).astype(BF16)
        total = total + dot_n(pick, cache_ref[tap])
    out_ref[...] = total
    shape = (slots, slots)
    bucket = iota(shape, 1)
    hit = (col != own) & (col == bucket // CAP) & (ranks_col(row, col, slots) == bucket % CAP)
    plan_ref[0:1, :] = jnp.sum(jnp.where(hit, iota(shape, 0) + 1, 0), axis=0, keepdims=True) - 1
    row = source_ref[...]
    col = as_column(row, slots)
    hit = (col != own) & (col == bucket // CAP) & (ranks_col(row, col, slots) == bucket % CAP)
    plan_ref[1:2, :] = jnp.sum(jnp.where(hit, iota(shape, 0) + 1, 0), axis=0, keepdims=True) - 1


def pick_state_kernel(plan_ref, state_ref, out_hbm, out_ref, sems, out_sem):
    buckets, states, _ = out_ref.shape
    copies = []
    for b in range(buckets):
        rows = pl.ds(pl.multiple_of(jnp.maximum(plan_ref[0, b], 0) * states, states), states)
        copies.append(pltpu.make_async_copy(state_ref.at[rows], out_ref.at[b], sems.at[b]))
    for copy in copies:
        copy.start()
    for copy in copies:
        copy.wait()
    copy = pltpu.make_async_copy(out_ref, out_hbm, out_sem.at[0])
    copy.start()
    copy.wait()


def conv_steps(window, taps_ref, bias, steps):
    taps = taps_ref[...].astype(F32)
    outs = []
    for t in range(steps):
        total = bias
        for k in range(taps.shape[0]):
            total = total + taps[k : k + 1, :] * window[t + k]
        outs.append(jax.nn.silu(total).astype(BF16))
    return outs


def conv_kernel(pos_ref, dest_hbm, source_hbm, active_hbm, both_ref, cache_hbm, taps_hbm, bias_hbm,
                conv_ref, z_out, cache_out_ref, arr_ref, sems,
                dest_ref, source_ref, active_ref, cache_ref, taps_ref, bias_ref, in_sems):
    x_ref = both_ref.at[0]
    copies = fetch(
        ((dest_hbm, dest_ref), (source_hbm, source_ref), (active_hbm, active_ref), (cache_hbm, cache_ref),
         (taps_hbm, taps_ref), (bias_hbm, bias_ref)),
        in_sems,
    )
    gate_copy = pltpu.make_async_copy(both_ref.at[1], z_out, sems.at[0])
    gate_copy.start()
    for copy in copies:
        copy.wait()
    steps, slots, width = x_ref.shape
    taps = cache_ref.shape[0]
    own = pos_ref[0]
    dest = as_column(dest_ref[...], slots)
    alive = as_column(active_ref[...], slots)
    step = 16
    for r in range(0, slots, step):
        rows = slice(r, r + step)
        keep = [cache_ref[j, rows, :] for j in range(taps)]
        new = [x_ref[t, rows, :] for t in range(steps)]
        outs = conv_steps([v.astype(F32) for v in keep + new], taps_ref, bias_ref[...], steps)
        for t in range(steps):
            conv_ref[t, rows, :] = outs[t]
        on = alive[rows, :] == 1
        gone = dest[rows, :] != own
        for j in range(taps):
            old = jnp.where(gone, 0.0, keep[j].astype(F32))
            cache_out_ref[j, rows, :] = jnp.where(on, new[j].astype(F32), old).astype(BF16)
    buckets = arr_ref.shape[0] // steps
    row = source_ref[...]
    rank = ranks_row(row, as_column(row, slots), slots)
    shape = (buckets, slots)
    hit = (row == iota(shape, 0) // CAP) & (row != own) & (rank == iota(shape, 0) % CAP)
    pick = jnp.where(hit, 1.0, 0.0).astype(BF16)
    for t in range(steps):
        arr_ref[t * buckets : (t + 1) * buckets, :] = dot_n(pick, x_ref[t]).astype(BF16)
    gate_copy.wait()


def project_kernel(pos_ref, source_ref, got_ref, arr_ref, conv_ref, taps_ref, bias_ref, proj_ref,
                   conv_out, a0, a1, a2, a3, b0, b1, b2, b3, conv_s, mix, low, sems):
    steps, slots, width = conv_ref.shape
    buckets = arr_ref.shape[0] // steps
    got = got_ref[...].astype(BF16)
    shape = (buckets, got.shape[0])
    window = []
    for j in range(taps_ref.shape[0] - 1):
        place = (iota(shape, 0) // CAP) * 8 + j * CAP + iota(shape, 0) % CAP
        window.append(dot_n(jnp.where(iota(shape, 1) == place, 1.0, 0.0).astype(BF16), got))
    for t in range(steps):
        window.append(arr_ref[t * buckets : (t + 1) * buckets, :].astype(F32))
    outs = conv_steps(window, taps_ref, bias_ref[...], steps)
    row = source_ref[...]
    col = as_column(row, slots)
    rank = ranks_col(row, col, slots)
    arriving = col != pos_ref[0]
    shape = (slots, buckets)
    hit = arriving & (col == iota(shape, 1) // CAP) & (rank == iota(shape, 1) % CAP)
    pick = jnp.where(hit, 1.0, 0.0).astype(BF16)
    for t in range(steps):
        moved = dot_n(pick, outs[t])
        conv_s[t * slots : (t + 1) * slots, :] = jnp.where(arriving, moved, conv_ref[t].astype(F32)).astype(BF16)
    copy = pltpu.make_async_copy(conv_s, conv_out, sems.at[0])
    copy.start()
    lhs = conv_s[...]
    mix[...] = dot_t(lhs, proj_ref[0:width, :])
    rest = proj_ref.shape[0] - width
    low[:, 0:rest] = dot_t(lhs, proj_ref[width:, :])
    quarter = slots // 2 // SIDE
    for half, outs in ((0, (a0, a1, a2, a3)), (1, (b0, b1, b2, b3))):
        for d in range(SIDE):
            q = lax.rem(pos_ref[1 + half] + d, SIDE)
            out = outs[d]
            out[steps * quarter :, :] = jnp.zeros((8, width), F32)
            for t in range(steps):
                start = pl.multiple_of(t * slots + half * (slots // 2) + q * quarter, quarter)
                out[t * quarter : (t + 1) * quarter, :] = mix[pl.ds(start, quarter), :]
                for g in range(quarter // 8):
                    lane = 32 * (t * (quarter // 8) + g)
                    out[steps * quarter :, lane : lane + rest] = low[pl.ds(start + 8 * g, 8), 0:rest]
    copy.wait()


def prepare(pos_ref, active_ref, pieces_x, pieces_y, conv_ref, dtw_ref, dtb_ref,
            step_ref, conv_out_ref, low_ref, rank_s, wait):
    total, width = conv_ref.shape
    slots = active_ref.shape[1]
    steps = total // slots
    quarter = slots // 2 // SIDE
    half = steps * quarter
    groups = quarter // 8
    rest = 32
    for axis, pieces in ((0, pieces_x), (1, pieces_y)):
        for d in range(SIDE):
            q = lax.rem(pos_ref[1 + axis] + (SIDE - d), SIDE)
            for t in range(steps):
                start = pl.multiple_of(t * slots + axis * (slots // 2) + q * quarter, quarter)
                rank_s[pl.ds(start, quarter), :] = pieces[d][t * quarter : (t + 1) * quarter, :].astype(BF16)
                for g in range(groups):
                    lane = 32 * (t * groups + g)
                    low_ref[pl.ds(start + 8 * g, 8), 0:rest] = pieces[d][half:, lane : lane + rest]
    alive = as_column(active_ref[...], slots) == 1
    wait()
    for t in range(steps):
        rows = slice(t * slots, (t + 1) * slots)
        conv_out_ref[rows, :] = conv_ref[rows, :].astype(F32)
        raw = dot_n(rank_s[rows, :], dtw_ref[...]) + dtb_ref[...]
        soft = jnp.maximum(raw, 0.0) + jnp.log1p(jnp.exp(-jnp.abs(raw)))
        step_ref[rows, :] = jnp.where(alive, soft, 0.0)


def scan_kernel(pos_ref, plan_ref, active_hbm, x0, x1, x2, x3, y0, y1, y2, y3, got_ref,
                conv_hbm, z_hbm, dtw_hbm, dtb_hbm, rate_hbm, gain_hbm, state_ref,
                gated_ref, out_ref, alive_s, rate_s, state_s, step_s, conv_s, low_s, rank_s,
                active_ref, conv_ref, z_ref, dtw_ref, dtb_ref, rate_ref, gain_ref,
                in_sems, out_sems, sems):
    steps, slots, width = z_ref.shape
    states = rate_ref.shape[0]
    block = slots // in_sems.shape[0]
    tiles = width // 128

    def load(i, l):
        rows = pl.ds(i * block * states, block * states)
        return pltpu.make_async_copy(state_ref.at[rows, pl.ds(l * 128, 128)], state_s.at[l, rows], in_sems.at[i, l])

    def store(i, l):
        rows = pl.ds(i * block * states, block * states)
        return pltpu.make_async_copy(state_s.at[l, rows], out_ref.at[rows, pl.ds(l * 128, 128)], out_sems.at[i, l])

    copies = fetch(
        ((active_hbm, active_ref), (dtw_hbm, dtw_ref), (dtb_hbm, dtb_ref), (conv_hbm, conv_ref),
         (rate_hbm, rate_ref), (gain_hbm, gain_ref), (z_hbm, z_ref)),
        sems,
    )
    for i in range(slots // block):
        for l in range(tiles):
            load(i, l).start()
    copies[0].wait()

    def ready():
        for copy in copies[1:]:
            copy.wait()

    prepare(pos_ref, active_ref, (x0, x1, x2, x3), (y0, y1, y2, y3), conv_ref, dtw_ref, dtb_ref,
            step_s, conv_s, low_s, rank_s, ready)
    rate_s[...] = rate_ref[...] * (-1.0 / math.log(2.0))
    alive = as_column(active_ref[...], slots) == 1
    alive_s[...] = jnp.broadcast_to(jnp.where(alive, 1.0, 0.0), alive_s.shape)
    for i in range(slots // block):
        for l in range(tiles):
            load(i, l).wait()
    buckets = got_ref.shape[0] // states

    def patch(b, carry):
        gone = plan_ref[0, b]
        here = plan_ref[1, b]

        @pl.when(gone >= 0)
        def _():
            rows = pl.ds(pl.multiple_of(gone * states, states), states)
            for l in range(tiles):
                state_s[l, rows, :] = jnp.zeros((states, 128), F32)

        @pl.when(here >= 0)
        def _():
            rows = pl.ds(pl.multiple_of(here * states, states), states)
            there = pl.ds(pl.multiple_of(b * states, states), states)
            for l in range(tiles):
                state_s[l, rows, :] = got_ref[there, l * 128 : (l + 1) * 128]

        return carry

    lax.fori_loop(0, buckets, patch, 0)

    def group(base):
        dts, dxs, lows, accs = [], [], [], []
        for t in range(steps):
            rows = pl.ds(pl.multiple_of(t * slots + base, 8), 8)
            lows.append(low_s[rows, :])
            for l in range(tiles):
                lanes = slice(l * 128, (l + 1) * 128)
                dt = step_s[rows, lanes]
                cv = conv_s[rows, lanes]
                dts.append(dt)
                dxs.append(dt * cv)
                accs.append(gain_ref[:, lanes] * cv)
        for n in range(states):
            place = pl.ds(base * states + n, 8, stride=states)
            gives = [jnp.broadcast_to(low[:, n : n + 1], (8, 128)) for low in lows]
            takes = [jnp.broadcast_to(low[:, states + n : states + n + 1], (8, 128)) for low in lows]
            for l in range(tiles):
                st = state_s[l, place, :]
                rate = rate_s[n : n + 1, l * 128 : (l + 1) * 128]
                for t in range(steps):
                    k = t * tiles + l
                    st = jnp.exp2(dts[k] * rate) * st + dxs[k] * gives[t]
                    accs[k] = accs[k] + st * takes[t]
                state_s[l, place, :] = st
        return accs

    def pair(i, carry):
        base = pl.multiple_of(i * 16, 16)
        accs = [group(base), group(pl.multiple_of(base + 8, 8))]
        on = alive_s[pl.ds(base, 16), :] > 0.5
        for t in range(steps):
            for l in range(tiles):
                lanes = slice(l * 128, (l + 1) * 128)
                gate = jax.nn.silu(z_ref[t, pl.ds(base, 16), lanes].astype(F32))
                value = jnp.concatenate([accs[0][t * tiles + l], accs[1][t * tiles + l]], axis=0) * gate
                gated_ref[t, pl.ds(base, 16), lanes] = jnp.where(on, value, 0.0).astype(BF16)
        return carry

    def chunk(i, carry):
        lax.fori_loop(i * (block // 16), (i + 1) * (block // 16), pair, 0)
        for l in range(tiles):
            store(i, l).start()
        return carry

    lax.fori_loop(0, slots // block, chunk, 0)
    for i in range(slots // block):
        for l in range(tiles):
            store(i, l).wait()


def in_hbm(value):
    return pltpu.with_memory_space_constraint(value, pltpu.HBM)


def on_device(projected, conv_weight, conv_bias, xproj_weight, dtproj_weight, dt_bias, a_rate, skip_gain,
              ssm_state, conv_cache, send_dest, recv_source, active):
    steps, slots, _, width = projected.shape
    rank_width = dtproj_weight.shape[0]
    states = a_rate.shape[0]
    taps = conv_weight.shape[0]
    peers = lax.axis_size("req")
    buckets = peers * CAP
    place = lax.axis_index("wa")
    pos = jnp.stack([lax.axis_index("req"), place // SIDE, place % SIDE]).astype(jnp.int32)
    send_row, recv_row, active_row = (in_hbm(v.reshape(1, slots)) for v in (send_dest, recv_source, active))
    recv_rows = recv_source.reshape(1, slots)
    bias, dt_row, gain = (v.reshape(1, width) for v in (conv_bias, dt_bias, skip_gain))
    cache = in_hbm(jnp.transpose(conv_cache, (1, 0, 2)))
    proj = jnp.transpose(xproj_weight, (1, 0))
    state_rows = in_hbm(ssm_state.reshape(slots * states, width))
    sds = jax.ShapeDtypeStruct

    out_cache, plan = pl.pallas_call(
        pick_cache_kernel,
        out_shape=(sds((peers * 8, width), F32), sds((2, slots), jnp.int32)),
        in_specs=[SM, HB, HB, HB],
        out_specs=(VM, VM),
        scratch_shapes=[
            pltpu.VMEM((1, slots), jnp.int32),
            pltpu.VMEM((1, slots), jnp.int32),
            pltpu.VMEM(cache.shape, BF16),
            pltpu.SemaphoreType.DMA((3,)),
        ],
        compiler_params=pltpu.CompilerParams(vmem_limit_bytes=4 * MIB),
        name="pick_cache",
    )(pos, send_row, recv_row, cache)
    both = jnp.transpose(projected, (2, 0, 1, 3))
    got_cache = lax.all_to_all(
        out_cache.reshape(peers, 8, width), "req", split_axis=0, concat_axis=0, tiled=True
    ).reshape(peers * 8, width)

    out_state = pl.pallas_call(
        pick_state_kernel,
        out_shape=pltpu.HBM((buckets, states, width), F32),
        in_specs=[SM, HB],
        out_specs=HB,
        scratch_shapes=[
            pltpu.VMEM((buckets, states, width), F32),
            pltpu.SemaphoreType.DMA((buckets,)),
            pltpu.SemaphoreType.DMA((1,)),
        ],
        cost_estimate=pl.CostEstimate(flops=1, bytes_accessed=1, transcendentals=0),
        compiler_params=pltpu.CompilerParams(vmem_limit_bytes=4 * MIB),
        name="pick_state",
    )(plan, state_rows)

    total = steps * slots
    conv_main, z_part, cache_out, x_arr = pl.pallas_call(
        conv_kernel,
        out_shape=(
            sds((steps, slots, width), BF16),
            pltpu.HBM((steps, slots, width), BF16),
            sds((taps - 1, slots, width), BF16),
            sds((steps * buckets, width), BF16),
        ),
        in_specs=[SM] + [HB] * 3 + [VM] + [HB] * 3,
        out_specs=(VM, HB, VM, VM),
        scratch_shapes=[
            pltpu.SemaphoreType.DMA((1,)),
            pltpu.VMEM((1, slots), jnp.int32),
            pltpu.VMEM((1, slots), jnp.int32),
            pltpu.VMEM((1, slots), jnp.int32),
            pltpu.VMEM(cache.shape, BF16),
            pltpu.VMEM(conv_weight.shape, BF16),
            pltpu.VMEM((1, width), F32),
            pltpu.SemaphoreType.DMA((6,)),
        ],
        compiler_params=pltpu.CompilerParams(vmem_limit_bytes=8 * MIB),
        name="convolve",
    )(pos, send_row, recv_row, active_row, both, cache, in_hbm(conv_weight), in_hbm(bias))

    out_state, conv_main, x_arr = lax.optimization_barrier((out_state, conv_main, x_arr))
    half = steps * (slots // 2 // SIDE)
    projected_parts = pl.pallas_call(
        project_kernel,
        out_shape=(pltpu.HBM((total, width), BF16),) + (sds((half + 8, width), F32),) * (2 * SIDE),
        in_specs=[SM] + [VM] * 7,
        out_specs=(HB,) + (VM,) * (2 * SIDE),
        scratch_shapes=[
            pltpu.VMEM((total, width), BF16),
            pltpu.VMEM((total, width), F32),
            pltpu.VMEM((total, 128), F32),
            pltpu.SemaphoreType.DMA((1,)),
        ],
        compiler_params=pltpu.CompilerParams(vmem_limit_bytes=8 * MIB),
        name="project",
    )(pos, recv_rows, got_cache, x_arr, conv_main, conv_weight, bias, proj)
    conv_all = projected_parts[0]
    own_a, own_b = projected_parts[1 : 1 + SIDE], projected_parts[1 + SIDE :]

    def gathered(value, axis, parts):
        return [value] + [lax.ppermute(parts[d - 1], "wa", shift(axis, d)) for d in range(1, SIDE)]

    def summed(value, axis, parts):
        pieces = gathered(value, axis, parts)
        return pieces[0] + pieces[1] + pieces[2] + pieces[3]

    sum_a = summed(own_a[0], 0, own_a[1:])
    sum_b = summed(own_b[0], 1, own_b[1:])
    got_state = lax.all_to_all(out_state, "req", split_axis=0, concat_axis=0, tiled=True)
    all_a = summed(sum_a, 1, [sum_a] * 3)
    all_b = summed(sum_b, 0, [sum_b] * 3)
    last_x = gathered(all_a, 0, [all_a] * 3)
    last_y = gathered(all_b, 1, [all_b] * 3)

    gated_out, state_out = pl.pallas_call(
        scan_kernel,
        out_shape=(sds((steps, slots, width), BF16), sds((slots * states, width), F32)),
        in_specs=[SM, SM, HB] + [VM] * 9 + [HB] * 7,
        out_specs=(VM, HB),
        scratch_shapes=[
            pltpu.VMEM((slots, 128), F32),
            pltpu.VMEM((states, width), F32),
            pltpu.VMEM((width // 128, slots * states, 128), F32),
            pltpu.VMEM((total, width), F32),
            pltpu.VMEM((total, width), F32),
            pltpu.VMEM((total, 128), F32),
            pltpu.VMEM((total, width), BF16),
            pltpu.VMEM((1, slots), jnp.int32),
            pltpu.VMEM((total, width), BF16),
            pltpu.VMEM((steps, slots, width), BF16),
            pltpu.VMEM(dtproj_weight.shape, BF16),
            pltpu.VMEM((1, width), F32),
            pltpu.VMEM((states, width), F32),
            pltpu.VMEM((1, width), F32),
            pltpu.SemaphoreType.DMA((4, width // 128)),
            pltpu.SemaphoreType.DMA((4, width // 128)),
            pltpu.SemaphoreType.DMA((7,)),
        ],
        compiler_params=pltpu.CompilerParams(vmem_limit_bytes=20 * MIB),
        name="scan",
    )(
        pos, plan, active_row, *last_x, *last_y, got_state.reshape(buckets * states, width),
        in_hbm(conv_all), in_hbm(z_part), in_hbm(dtproj_weight), in_hbm(dt_row),
        in_hbm(a_rate), in_hbm(gain), state_rows,
    )
    return (
        gated_out,
        state_out.reshape(slots, states, width),
        jnp.transpose(cache_out, (1, 0, 2)),
    )


def solution(mesh):
    return jax.shard_map(
        on_device,
        mesh=mesh,
        in_specs=(
            P(None, "req", None, "wa"),
            P(None, "wa"),
            P("wa"),
            P("wa", None),
            P(None, "wa"),
            P("wa"),
            P(None, "wa"),
            P("wa"),
            P("req", None, "wa"),
            P("req", None, "wa"),
            P("req"),
            P("req"),
            P("req"),
        ),
        out_specs=(P(None, "req", "wa"), P("req", None, "wa"), P("req", None, "wa")),
        check_vma=False,
    )
```

```python
import math

import jax
import jax.numpy as jnp
from jax import lax
from jax.experimental import pallas as pl
from jax.experimental.pallas import tpu as pltpu
from jax.sharding import PartitionSpec as P

CAP = 2
SIDE = 4
MIB = 1 << 20
F32 = jnp.float32
BF16 = jnp.bfloat16
VM = pl.BlockSpec(memory_space=pltpu.VMEM)
SM = pl.BlockSpec(memory_space=pltpu.SMEM)
HB = pl.BlockSpec(memory_space=pltpu.HBM)


def shift(axis, amount):
    pairs = []
    for x in range(SIDE):
        for y in range(SIDE):
            tx, ty = (x + amount) % SIDE, y
            if axis == 1:
                tx, ty = x, (y + amount) % SIDE
            pairs.append((x * SIDE + y, tx * SIDE + ty))
    return pairs


def dot_t(lhs, rhs):
    return lax.dot_general(lhs, rhs, (((1,), (1,)), ((), ())), preferred_element_type=F32)


def dot_n(lhs, rhs):
    return jnp.dot(lhs, rhs, preferred_element_type=F32)


def iota(shape, dim):
    return lax.broadcasted_iota(jnp.int32, shape, dim)


def as_column(row, size):
    eye = iota((size, size), 0) == iota((size, size), 1)
    return jnp.sum(jnp.where(eye, jnp.broadcast_to(row, (size, size)), 0), axis=1, keepdims=True)


def ranks_row(row, col, size):
    earlier = (col == row) & (iota((size, size), 0) < iota((size, size), 1))
    return jnp.sum(jnp.where(earlier, 1, 0), axis=0, keepdims=True)


def ranks_col(row, col, size):
    earlier = (col == row) & (iota((size, size), 1) < iota((size, size), 0))
    return jnp.sum(jnp.where(earlier, 1, 0), axis=1, keepdims=True)


def fetch(pairs, sems):
    copies = [pltpu.make_async_copy(a, b, sems.at[i]) for i, (a, b) in enumerate(pairs)]
    for copy in copies:
        copy.start()
    return copies


def pick_cache_kernel(pos_ref, dest_hbm, source_hbm, cache_hbm, out_ref, plan_ref, dest_ref, source_ref, cache_ref,
                      full_s, sems):
    copies = fetch(((dest_hbm, dest_ref), (source_hbm, source_ref), (cache_hbm, cache_ref)), sems)
    for copy in copies[:2]:
        copy.wait()
    taps, slots, _ = cache_ref.shape
    own = pos_ref[0]
    row = dest_ref[...]
    col = as_column(row, slots)
    rank = ranks_row(row, col, slots)
    rows = full_s.shape[0]
    shape = (rows, slots)
    target = iota(shape, 0) // 8
    place = iota(shape, 0) % 8
    total = jnp.zeros(full_s.shape, F32)
    square = (slots, slots)
    bucket = iota(square, 1)
    for k, ref in enumerate((dest_ref, source_ref)):
        plan_row = ref[...]
        plan_col = as_column(plan_row, slots)
        hit = (plan_col != own) & (plan_col == bucket // CAP) & (ranks_col(plan_row, plan_col, slots) == bucket % CAP)
        plan_ref[k : k + 1, :] = jnp.sum(jnp.where(hit, iota(square, 0) + 1, 0), axis=0, keepdims=True) - 1
    copies[2].wait()
    hit = (row == target) & (row != own) & (rank == place % CAP)
    for tap in range(taps):
        pick = jnp.where(hit & (place // CAP == tap), 1.0, 0.0).astype(BF16)
        total = total + dot_n(pick, cache_ref[tap])
    full_s[...] = total
    used = taps * CAP
    tiles = full_s.shape[1] // 128
    for d in range(rows // 8):
        for l in range(tiles):
            start = (d * tiles + l) * used
            out_ref[start : start + used, :] = full_s[8 * d : 8 * d + used, l * 128 : (l + 1) * 128]


def pick_state_kernel(plan_ref, state_ref, out_hbm, out_ref, sems, out_sem):
    buckets, states, _ = out_ref.shape
    copies = []
    for b in range(buckets):
        rows = pl.ds(pl.multiple_of(jnp.maximum(plan_ref[0, b], 0) * states, states), states)
        copies.append(pltpu.make_async_copy(state_ref.at[rows], out_ref.at[b], sems.at[b]))
    for copy in copies:
        copy.start()
    for copy in copies:
        copy.wait()
    copy = pltpu.make_async_copy(out_ref, out_hbm, out_sem.at[0])
    copy.start()
    copy.wait()


def conv_steps(window, taps_ref, bias, steps):
    taps = taps_ref[...].astype(F32)
    outs = []
    for t in range(steps):
        total = bias
        for k in range(taps.shape[0]):
            total = total + taps[k : k + 1, :] * window[t + k]
        outs.append(jax.nn.silu(total).astype(BF16))
    return outs


def conv_kernel(pos_ref, dest_hbm, source_hbm, active_hbm, both_ref, cache_hbm, taps_hbm, bias_hbm,
                conv_ref, gate_out, cache_out_ref, arr_ref, sems,
                dest_ref, source_ref, active_ref, cache_ref, taps_ref, bias_ref, in_sems):
    x_ref = both_ref.at[0]
    copies = fetch(
        ((dest_hbm, dest_ref), (source_hbm, source_ref), (active_hbm, active_ref), (cache_hbm, cache_ref),
         (taps_hbm, taps_ref), (bias_hbm, bias_ref)),
        in_sems,
    )
    gate_copy = pltpu.make_async_copy(both_ref.at[1], gate_out, sems.at[0])
    gate_copy.start()
    for copy in copies:
        copy.wait()
    steps, slots, width = x_ref.shape
    taps = cache_ref.shape[0]
    own = pos_ref[0]
    dest = as_column(dest_ref[...], slots)
    alive = as_column(active_ref[...], slots)
    step = 16
    for r in range(0, slots, step):
        rows = slice(r, r + step)
        keep = [cache_ref[j, rows, :] for j in range(taps)]
        new = [x_ref[t, rows, :] for t in range(steps)]
        outs = conv_steps([v.astype(F32) for v in keep + new], taps_ref, bias_ref[...], steps)
        for t in range(steps):
            conv_ref[t, rows, :] = outs[t]
        on = alive[rows, :] == 1
        gone = dest[rows, :] != own
        for j in range(taps):
            old = jnp.where(gone, 0.0, keep[j].astype(F32))
            cache_out_ref[j, rows, :] = jnp.where(on, new[j].astype(F32), old).astype(BF16)
    buckets = arr_ref.shape[0] // steps
    row = source_ref[...]
    rank = ranks_row(row, as_column(row, slots), slots)
    shape = (buckets, slots)
    hit = (row == iota(shape, 0) // CAP) & (row != own) & (rank == iota(shape, 0) % CAP)
    pick = jnp.where(hit, 1.0, 0.0).astype(BF16)
    for t in range(steps):
        arr_ref[t * buckets : (t + 1) * buckets, :] = dot_n(pick, x_ref[t]).astype(BF16)
    gate_copy.wait()


def project_kernel(pos_ref, source_ref, got_ref, arr_ref, conv_ref, taps_ref, bias_ref, proj_ref,
                   conv_out, a0, a1, a2, a3, b0, b1, b2, b3, mix, low, full_s, conv_s, sems):
    steps, slots, width = conv_ref.shape
    buckets = arr_ref.shape[0] // steps
    used = (taps_ref.shape[0] - 1) * CAP
    tiles = width // 128
    full_s[...] = jnp.zeros(full_s.shape, F32)
    for d in range(full_s.shape[0] // 8):
        for l in range(tiles):
            start = (d * tiles + l) * used
            full_s[8 * d : 8 * d + used, l * 128 : (l + 1) * 128] = got_ref[start : start + used, :]
    got = full_s[...].astype(BF16)
    shape = (buckets, got.shape[0])
    window = []
    for j in range(taps_ref.shape[0] - 1):
        place = (iota(shape, 0) // CAP) * 8 + j * CAP + iota(shape, 0) % CAP
        window.append(dot_n(jnp.where(iota(shape, 1) == place, 1.0, 0.0).astype(BF16), got))
    for t in range(steps):
        window.append(arr_ref[t * buckets : (t + 1) * buckets, :].astype(F32))
    outs = conv_steps(window, taps_ref, bias_ref[...], steps)
    row = source_ref[...]
    col = as_column(row, slots)
    rank = ranks_col(row, col, slots)
    arriving = col != pos_ref[0]
    shape = (slots, buckets)
    hit = arriving & (col == iota(shape, 1) // CAP) & (rank == iota(shape, 1) % CAP)
    pick = jnp.where(hit, 1.0, 0.0).astype(BF16)
    copies = []
    for t in range(steps):
        moved = dot_n(pick, outs[t])
        rows = pl.ds(t * slots, slots)
        conv_s[rows, :] = jnp.where(arriving, moved, conv_ref[t].astype(F32)).astype(BF16)
        copies.append(pltpu.make_async_copy(conv_s.at[rows], conv_out.at[rows], sems.at[t]))
        copies[t].start()
    lhs = conv_s[...]
    mix[...] = dot_t(lhs, proj_ref[0:width, :])
    rest = proj_ref.shape[0] - width
    low[:, 0:rest] = dot_t(lhs, proj_ref[width:, :])
    quarter = slots // 2 // SIDE
    for half, outs in ((0, (a0, a1, a2, a3)), (1, (b0, b1, b2, b3))):
        for d in range(SIDE):
            q = lax.rem(pos_ref[1 + half] + d, SIDE)
            out = outs[d]
            out[steps * quarter :, :] = jnp.zeros((8, width), F32)
            for t in range(steps):
                start = pl.multiple_of(t * slots + half * (slots // 2) + q * quarter, quarter)
                out[t * quarter : (t + 1) * quarter, :] = mix[pl.ds(start, quarter), :]
                for g in range(quarter // 8):
                    lane = 32 * (t * (quarter // 8) + g)
                    out[steps * quarter :, lane : lane + rest] = low[pl.ds(start + 8 * g, 8), 0:rest]
    for copy in copies:
        copy.wait()


def prepare(pos_ref, active_ref, pieces_x, pieces_y, conv_ref, dtw_ref, dtb_ref,
            step_ref, conv_out_ref, low_ref, rank_s, wait):
    total, width = conv_ref.shape
    slots = active_ref.shape[1]
    steps = total // slots
    quarter = slots // 2 // SIDE
    half = steps * quarter
    groups = quarter // 8
    rest = 32
    for axis, pieces in ((0, pieces_x), (1, pieces_y)):
        for d in range(SIDE):
            q = lax.rem(pos_ref[1 + axis] + (SIDE - d), SIDE)
            for t in range(steps):
                start = pl.multiple_of(t * slots + axis * (slots // 2) + q * quarter, quarter)
                rank_s[pl.ds(start, quarter), :] = pieces[d][t * quarter : (t + 1) * quarter, :].astype(BF16)
                for g in range(groups):
                    lane = 32 * (t * groups + g)
                    low_ref[pl.ds(start + 8 * g, 8), 0:rest] = pieces[d][half:, lane : lane + rest]
    alive = as_column(active_ref[...], slots) == 1
    wait()
    for t in range(steps):
        rows = slice(t * slots, (t + 1) * slots)
        conv_out_ref[rows, :] = conv_ref[rows, :].astype(F32)
        raw = dot_n(rank_s[rows, :], dtw_ref[...]) + dtb_ref[...]
        soft = jnp.maximum(raw, 0.0) + jnp.log1p(jnp.exp(-jnp.abs(raw)))
        step_ref[rows, :] = jnp.where(alive, soft, 0.0)


def stage_kernel(plan_ref, got_ref, state_ref, out_ref, spread_ref, sems):
    tiles, rows, _ = out_ref.shape
    buckets = sems.shape[1]
    states = got_ref.shape[0] // buckets
    parts = sems.shape[0]
    copies = []
    for l in range(tiles):
        for i in range(parts):
            here = pl.ds(i * (rows // parts), rows // parts)
            copies.append(
                pltpu.make_async_copy(state_ref.at[here, pl.ds(l * 128, 128)], out_ref.at[l, here], sems.at[i, l])
            )
    for copy in copies:
        copy.start()
    shape = spread_ref.shape
    spread_ref[...] = jnp.where(iota(shape, 0) % (shape[0] // 2) == iota(shape, 1) // 128, 1.0, 0.0).astype(BF16)
    for copy in copies:
        copy.wait()

    def patch(b, carry):
        gone = plan_ref[0, b]
        here = plan_ref[1, b]

        @pl.when(gone >= 0)
        def _():
            rows = pl.ds(pl.multiple_of(gone * states, states), states)
            for l in range(tiles):
                out_ref[l, rows, :] = jnp.zeros((states, 128), F32)

        @pl.when(here >= 0)
        def _():
            rows = pl.ds(pl.multiple_of(here * states, states), states)
            there = pl.ds(pl.multiple_of(b * states, states), states)
            for l in range(tiles):
                out_ref[l, rows, :] = got_ref[there, l * 128 : (l + 1) * 128]

        return carry

    lax.fori_loop(0, buckets, patch, 0)


PIECES = (48, 32, 16, 16, 16)


def scan_kernel(pos_ref, active_ref, x0, x1, x2, x3, y0, y1, y2, y3, state_s,
                spread_ref, conv_ref, gate_ref, dtw_ref, dtb_ref, rate_ref, gain_ref,
                gated_out, out_ref, alive_s, rate_s, final_s, step_s, conv_s, low_s, rank_s, gated_ref, wide_s,
                out_sems):
    steps, slots, width = gate_ref.shape
    states = rate_ref.shape[0]
    tiles = width // 128

    def stores(k):
        first = sum(PIECES[:k])
        slots_here = pl.ds(first, PIECES[k])
        rows = pl.ds(first * states, PIECES[k] * states)
        copies = [pltpu.make_async_copy(gated_ref.at[:, slots_here], gated_out.at[:, slots_here], out_sems.at[k, tiles])]
        for l in range(tiles):
            copies.append(
                pltpu.make_async_copy(final_s.at[l, rows], out_ref.at[rows, pl.ds(l * 128, 128)], out_sems.at[k, l])
            )
        return copies

    def ready():
        pass

    prepare(pos_ref, active_ref, (x0, x1, x2, x3), (y0, y1, y2, y3), conv_ref, dtw_ref, dtb_ref,
            step_s, conv_s, low_s, rank_s, ready)
    rest = 2 * states
    high = low_s[:, 0:rest].astype(BF16)
    rounding = (low_s[:, 0:rest] - high.astype(F32)).astype(BF16)
    wide_s[...] = dot_n(jnp.concatenate([high, rounding], axis=1), spread_ref[...])
    rate_s[...] = rate_ref[...] * (-1.0 / math.log(2.0))
    alive = as_column(active_ref[...], slots) == 1
    alive_s[...] = jnp.broadcast_to(jnp.where(alive, 1.0, 0.0), alive_s.shape)

    def group(base):
        dts, dxs, lows, accs = [], [], [], []
        for t in range(steps):
            rows = pl.ds(pl.multiple_of(t * slots + base, 8), 8)
            lows.append(rows)
            for l in range(tiles):
                lanes = slice(l * 128, (l + 1) * 128)
                dt = step_s[rows, lanes]
                cv = conv_s[rows, lanes]
                dts.append(dt)
                dxs.append(dt * cv)
                accs.append(gain_ref[:, lanes] * cv)
        for n in range(states):
            place = pl.ds(base * states + n, 8, stride=states)
            gives = [wide_s[rows, n * 128 : (n + 1) * 128] for rows in lows]
            takes = [wide_s[rows, (states + n) * 128 : (states + n + 1) * 128] for rows in lows]
            for l in range(tiles):
                st = state_s[l, place, :]
                rate = rate_s[n : n + 1, l * 128 : (l + 1) * 128]
                for t in range(steps):
                    k = t * tiles + l
                    st = jnp.exp2(dts[k] * rate) * st + dxs[k] * gives[t]
                    accs[k] = accs[k] + st * takes[t]
                final_s[l, place, :] = st
        return accs

    def pair(i, carry):
        base = pl.multiple_of(i * 16, 16)
        accs = [group(base), group(pl.multiple_of(base + 8, 8))]
        on = alive_s[pl.ds(base, 16), :] > 0.5
        for t in range(steps):
            for l in range(tiles):
                lanes = slice(l * 128, (l + 1) * 128)
                gate = jax.nn.silu(gate_ref[t, pl.ds(base, 16), lanes].astype(F32))
                value = jnp.concatenate([accs[0][t * tiles + l], accs[1][t * tiles + l]], axis=0) * gate
                gated_ref[t, pl.ds(base, 16), lanes] = jnp.where(on, value, 0.0).astype(BF16)
        return carry

    def block(i, carry):
        pair(i, carry)
        for k in range(len(PIECES)):

            @pl.when(i == sum(PIECES[: k + 1]) // 16 - 1)
            def _():
                for copy in stores(k):
                    copy.start()

        return carry

    lax.fori_loop(0, slots // 16, block, 0)
    for k in range(len(PIECES)):
        for copy in stores(k):
            copy.wait()


def in_hbm(value):
    return pltpu.with_memory_space_constraint(value, pltpu.HBM)


def on_device(projected, conv_weight, conv_bias, xproj_weight, dtproj_weight, dt_bias, a_rate, skip_gain,
              ssm_state, conv_cache, send_dest, recv_source, active):
    steps, slots, _, width = projected.shape
    rank_width = dtproj_weight.shape[0]
    states = a_rate.shape[0]
    taps = conv_weight.shape[0]
    peers = lax.axis_size("req")
    buckets = peers * CAP
    place = lax.axis_index("wa")
    pos = jnp.stack([lax.axis_index("req"), place // SIDE, place % SIDE]).astype(jnp.int32)
    send_row, recv_row, active_row = (in_hbm(v.reshape(1, slots)) for v in (send_dest, recv_source, active))
    recv_rows = recv_source.reshape(1, slots)
    bias, dt_row, gain = (v.reshape(1, width) for v in (conv_bias, dt_bias, skip_gain))
    cache = in_hbm(jnp.transpose(conv_cache, (1, 0, 2)))
    proj = jnp.transpose(xproj_weight, (1, 0))
    state_rows = in_hbm(ssm_state.reshape(slots * states, width))
    sds = jax.ShapeDtypeStruct

    compact = (taps - 1) * CAP * (width // 128)
    out_cache, plan = pl.pallas_call(
        pick_cache_kernel,
        out_shape=(sds((peers * compact, 128), F32), sds((2, slots), jnp.int32)),
        in_specs=[SM, HB, HB, HB],
        out_specs=(VM, VM),
        scratch_shapes=[
            pltpu.VMEM((1, slots), jnp.int32),
            pltpu.VMEM((1, slots), jnp.int32),
            pltpu.VMEM(cache.shape, BF16),
            pltpu.VMEM((peers * 8, width), F32),
            pltpu.SemaphoreType.DMA((3,)),
        ],
        compiler_params=pltpu.CompilerParams(vmem_limit_bytes=4 * MIB),
        name="pick_cache",
    )(pos, send_row, recv_row, cache)
    both = jnp.transpose(projected, (2, 0, 1, 3))
    got_cache = lax.all_to_all(
        out_cache.reshape(peers, compact, 128), "req", split_axis=0, concat_axis=0, tiled=True
    ).reshape(peers * compact, 128)

    out_state = pl.pallas_call(
        pick_state_kernel,
        out_shape=pltpu.HBM((buckets, states, width), F32),
        in_specs=[SM, HB],
        out_specs=HB,
        scratch_shapes=[
            pltpu.VMEM((buckets, states, width), F32),
            pltpu.SemaphoreType.DMA((buckets,)),
            pltpu.SemaphoreType.DMA((1,)),
        ],
        cost_estimate=pl.CostEstimate(flops=1, bytes_accessed=1, transcendentals=0),
        compiler_params=pltpu.CompilerParams(vmem_limit_bytes=4 * MIB),
        name="pick_state",
    )(plan, state_rows)

    total = steps * slots
    conv_main, gate, cache_out, x_arr = pl.pallas_call(
        conv_kernel,
        out_shape=(
            sds((steps, slots, width), BF16),
            pltpu.HBM((steps, slots, width), BF16),
            sds((taps - 1, slots, width), BF16),
            sds((steps * buckets, width), BF16),
        ),
        in_specs=[SM] + [HB] * 3 + [VM] + [HB] * 3,
        out_specs=(VM, HB, VM, VM),
        scratch_shapes=[
            pltpu.SemaphoreType.DMA((1,)),
            pltpu.VMEM((1, slots), jnp.int32),
            pltpu.VMEM((1, slots), jnp.int32),
            pltpu.VMEM((1, slots), jnp.int32),
            pltpu.VMEM(cache.shape, BF16),
            pltpu.VMEM(conv_weight.shape, BF16),
            pltpu.VMEM((1, width), F32),
            pltpu.SemaphoreType.DMA((6,)),
        ],
        compiler_params=pltpu.CompilerParams(vmem_limit_bytes=8 * MIB),
        name="convolve",
    )(pos, send_row, recv_row, active_row, both, cache, in_hbm(conv_weight), in_hbm(bias))

    out_state, conv_main, x_arr = lax.optimization_barrier((out_state, conv_main, x_arr))
    half = steps * (slots // 2 // SIDE)
    projected_parts = pl.pallas_call(
        project_kernel,
        out_shape=(pltpu.HBM((total, width), BF16),) + (sds((half + 8, width), F32),) * (2 * SIDE),
        in_specs=[SM] + [VM] * 7,
        out_specs=(HB,) + (VM,) * (2 * SIDE),
        scratch_shapes=[
            pltpu.VMEM((total, width), F32),
            pltpu.VMEM((total, 128), F32),
            pltpu.VMEM((peers * 8, width), F32),
            pltpu.VMEM((total, width), BF16),
            pltpu.SemaphoreType.DMA((3,)),
        ],
        compiler_params=pltpu.CompilerParams(vmem_limit_bytes=8 * MIB),
        name="project",
    )(pos, recv_rows, got_cache, x_arr, conv_main, conv_weight, bias, proj)
    conv_all = projected_parts[0]
    own_a, own_b = projected_parts[1 : 1 + SIDE], projected_parts[1 + SIDE :]

    def gathered(value, axis, parts):
        return [value] + [lax.ppermute(parts[d - 1], "wa", shift(axis, d)) for d in range(1, SIDE)]

    def summed(value, axis, parts):
        pieces = gathered(value, axis, parts)
        return pieces[0] + pieces[1] + pieces[2] + pieces[3]

    sum_a = summed(own_a[0], 0, own_a[1:])
    sum_b = summed(own_b[0], 1, own_b[1:])
    got_state = lax.all_to_all(out_state, "req", split_axis=0, concat_axis=0, tiled=True)
    all_a = summed(sum_a, 1, [sum_a] * 3)
    all_b = summed(sum_b, 0, [sum_b] * 3)
    last_x = gathered(all_a, 0, [all_a] * 3)
    last_y = gathered(all_b, 1, [all_b] * 3)

    tiles = width // 128
    staged, spread = pl.pallas_call(
        stage_kernel,
        out_shape=(sds((tiles, slots * states, 128), F32), sds((4 * states, 2 * states * 128), BF16)),
        in_specs=[SM, VM, HB],
        out_specs=(VM, VM),
        scratch_shapes=[pltpu.SemaphoreType.DMA((1, buckets))],
        compiler_params=pltpu.CompilerParams(vmem_limit_bytes=8 * MIB),
        cost_estimate=pl.CostEstimate(flops=0, bytes_accessed=12 * MIB, transcendentals=0),
        name="stage_state",
    )(plan, got_state.reshape(buckets * states, width), state_rows)

    gated_out, state_out = pl.pallas_call(
        scan_kernel,
        out_shape=(sds((steps, slots, width), BF16), sds((slots * states, width), F32)),
        in_specs=[SM] + [VM] * 17,
        out_specs=(HB, HB),
        scratch_shapes=[
            pltpu.VMEM((slots, 128), F32),
            pltpu.VMEM((states, width), F32),
            pltpu.VMEM((tiles, slots * states, 128), F32),
            pltpu.VMEM((total, width), F32),
            pltpu.VMEM((total, width), F32),
            pltpu.VMEM((total, 128), F32),
            pltpu.VMEM((total, width), BF16),
            pltpu.VMEM((steps, slots, width), BF16),
            pltpu.VMEM((total, 2 * states * 128), F32),
            pltpu.SemaphoreType.DMA((len(PIECES), tiles + 1)),
        ],
        compiler_params=pltpu.CompilerParams(vmem_limit_bytes=20 * MIB),
        name="scan",
    )(
        pos, active.reshape(1, slots), *last_x, *last_y, staged, spread, conv_all, gate, dtproj_weight, dt_row,
        a_rate, gain,
    )
    return (
        gated_out,
        state_out.reshape(slots, states, width),
        jnp.transpose(cache_out, (1, 0, 2)),
    )


def solution(mesh):
    return jax.shard_map(
        on_device,
        mesh=mesh,
        in_specs=(
            P(None, "req", None, "wa"),
            P(None, "wa"),
            P("wa"),
            P("wa", None),
            P(None, "wa"),
            P("wa"),
            P(None, "wa"),
            P("wa"),
            P("req", None, "wa"),
            P("req", None, "wa"),
            P("req"),
            P("req"),
            P("req"),
        ),
        out_specs=(P(None, "req", "wa"), P("req", None, "wa"), P("req", None, "wa")),
        check_vma=False,
    )
```

```python
import math

import jax
import jax.numpy as jnp
from jax import lax
from jax.experimental import pallas as pl
from jax.experimental.pallas import tpu as pltpu
from jax.sharding import PartitionSpec as P

CAP = 2
SIDE = 4
MIB = 1 << 20
F32 = jnp.float32
BF16 = jnp.bfloat16
VM = pl.BlockSpec(memory_space=pltpu.VMEM)
SM = pl.BlockSpec(memory_space=pltpu.SMEM)
HB = pl.BlockSpec(memory_space=pltpu.HBM)


def shift(axis, amount):
    pairs = []
    for x in range(SIDE):
        for y in range(SIDE):
            tx, ty = (x + amount) % SIDE, y
            if axis == 1:
                tx, ty = x, (y + amount) % SIDE
            pairs.append((x * SIDE + y, tx * SIDE + ty))
    return pairs


def dot_t(lhs, rhs):
    return lax.dot_general(lhs, rhs, (((1,), (1,)), ((), ())), preferred_element_type=F32)


def dot_n(lhs, rhs):
    return jnp.dot(lhs, rhs, preferred_element_type=F32)


def iota(shape, dim):
    return lax.broadcasted_iota(jnp.int32, shape, dim)


def as_column(row, size):
    eye = iota((size, size), 0) == iota((size, size), 1)
    return jnp.sum(jnp.where(eye, jnp.broadcast_to(row, (size, size)), 0), axis=1, keepdims=True)


def ranks_row(row, col, size):
    earlier = (col == row) & (iota((size, size), 0) < iota((size, size), 1))
    return jnp.sum(jnp.where(earlier, 1, 0), axis=0, keepdims=True)


def ranks_col(row, col, size):
    earlier = (col == row) & (iota((size, size), 1) < iota((size, size), 0))
    return jnp.sum(jnp.where(earlier, 1, 0), axis=1, keepdims=True)


def fetch(pairs, sems):
    copies = [pltpu.make_async_copy(a, b, sems.at[i]) for i, (a, b) in enumerate(pairs)]
    for copy in copies:
        copy.start()
    return copies


def pick_cache_kernel(pos_ref, dest_hbm, source_hbm, cache_hbm, out_ref, plan_ref, dest_ref, source_ref, cache_ref,
                      full_s, sems):
    copies = fetch(((dest_hbm, dest_ref), (source_hbm, source_ref), (cache_hbm, cache_ref)), sems)
    for copy in copies[:2]:
        copy.wait()
    taps, slots, _ = cache_ref.shape
    own = pos_ref[0]
    row = dest_ref[...]
    col = as_column(row, slots)
    rank = ranks_row(row, col, slots)
    rows = full_s.shape[0]
    shape = (rows, slots)
    target = iota(shape, 0) // 8
    place = iota(shape, 0) % 8
    total = jnp.zeros(full_s.shape, F32)
    square = (slots, slots)
    bucket = iota(square, 1)
    for k, ref in enumerate((dest_ref, source_ref)):
        plan_row = ref[...]
        plan_col = as_column(plan_row, slots)
        hit = (plan_col != own) & (plan_col == bucket // CAP) & (ranks_col(plan_row, plan_col, slots) == bucket % CAP)
        plan_ref[k : k + 1, :] = jnp.sum(jnp.where(hit, iota(square, 0) + 1, 0), axis=0, keepdims=True) - 1
    copies[2].wait()
    hit = (row == target) & (row != own) & (rank == place % CAP)
    for tap in range(taps):
        pick = jnp.where(hit & (place // CAP == tap), 1.0, 0.0).astype(BF16)
        total = total + dot_n(pick, cache_ref[tap])
    full_s[...] = total
    used = taps * CAP
    tiles = full_s.shape[1] // 128
    for d in range(rows // 8):
        for l in range(tiles):
            start = (d * tiles + l) * used
            out_ref[start : start + used, :] = full_s[8 * d : 8 * d + used, l * 128 : (l + 1) * 128]


def pick_state_kernel(plan_ref, state_ref, out_hbm, out_ref, sems, out_sem):
    buckets, states, _ = out_ref.shape
    copies = []
    for b in range(buckets):
        rows = pl.ds(pl.multiple_of(jnp.maximum(plan_ref[0, b], 0) * states, states), states)
        copies.append(pltpu.make_async_copy(state_ref.at[rows], out_ref.at[b], sems.at[b]))
    for copy in copies:
        copy.start()
    for copy in copies:
        copy.wait()
    copy = pltpu.make_async_copy(out_ref, out_hbm, out_sem.at[0])
    copy.start()
    copy.wait()


def conv_steps(window, taps_ref, bias, steps):
    taps = taps_ref[...].astype(F32)
    outs = []
    for t in range(steps):
        total = bias
        for k in range(taps.shape[0]):
            total = total + taps[k : k + 1, :] * window[t + k]
        outs.append(jax.nn.silu(total).astype(BF16))
    return outs


def conv_kernel(pos_ref, dest_hbm, source_hbm, active_hbm, both_ref, cache_hbm, taps_hbm, bias_hbm,
                conv_ref, gate_out, cache_out_ref, arr_ref, sems,
                dest_ref, source_ref, active_ref, cache_ref, taps_ref, bias_ref, in_sems):
    x_ref = both_ref.at[0]
    copies = fetch(
        ((dest_hbm, dest_ref), (source_hbm, source_ref), (active_hbm, active_ref), (cache_hbm, cache_ref),
         (taps_hbm, taps_ref), (bias_hbm, bias_ref)),
        in_sems,
    )
    gate_copy = pltpu.make_async_copy(both_ref.at[1], gate_out, sems.at[0])
    gate_copy.start()
    for copy in copies:
        copy.wait()
    steps, slots, width = x_ref.shape
    taps = cache_ref.shape[0]
    own = pos_ref[0]
    dest = as_column(dest_ref[...], slots)
    alive = as_column(active_ref[...], slots)
    step = 16
    for r in range(0, slots, step):
        rows = slice(r, r + step)
        keep = [cache_ref[j, rows, :] for j in range(taps)]
        new = [x_ref[t, rows, :] for t in range(steps)]
        outs = conv_steps([v.astype(F32) for v in keep + new], taps_ref, bias_ref[...], steps)
        for t in range(steps):
            conv_ref[t, rows, :] = outs[t]
        on = alive[rows, :] == 1
        gone = dest[rows, :] != own
        for j in range(taps):
            old = jnp.where(gone, 0.0, keep[j].astype(F32))
            cache_out_ref[j, rows, :] = jnp.where(on, new[j].astype(F32), old).astype(BF16)
    buckets = arr_ref.shape[0] // steps
    row = source_ref[...]
    rank = ranks_row(row, as_column(row, slots), slots)
    shape = (buckets, slots)
    hit = (row == iota(shape, 0) // CAP) & (row != own) & (rank == iota(shape, 0) % CAP)
    pick = jnp.where(hit, 1.0, 0.0).astype(BF16)
    for t in range(steps):
        arr_ref[t * buckets : (t + 1) * buckets, :] = dot_n(pick, x_ref[t]).astype(BF16)
    gate_copy.wait()


def project_kernel(pos_ref, source_ref, got_ref, arr_ref, conv_ref, taps_ref, bias_ref, proj_ref,
                   conv_out, a0, a1, a2, a3, b0, b1, b2, b3, mix, low, full_s, conv_s, sems):
    steps, slots, width = conv_ref.shape
    buckets = arr_ref.shape[0] // steps
    used = (taps_ref.shape[0] - 1) * CAP
    tiles = width // 128
    full_s[...] = jnp.zeros(full_s.shape, F32)
    for d in range(full_s.shape[0] // 8):
        for l in range(tiles):
            start = (d * tiles + l) * used
            full_s[8 * d : 8 * d + used, l * 128 : (l + 1) * 128] = got_ref[start : start + used, :]
    got = full_s[...].astype(BF16)
    shape = (buckets, got.shape[0])
    window = []
    for j in range(taps_ref.shape[0] - 1):
        place = (iota(shape, 0) // CAP) * 8 + j * CAP + iota(shape, 0) % CAP
        window.append(dot_n(jnp.where(iota(shape, 1) == place, 1.0, 0.0).astype(BF16), got))
    for t in range(steps):
        window.append(arr_ref[t * buckets : (t + 1) * buckets, :].astype(F32))
    outs = conv_steps(window, taps_ref, bias_ref[...], steps)
    row = source_ref[...]
    col = as_column(row, slots)
    rank = ranks_col(row, col, slots)
    arriving = col != pos_ref[0]
    shape = (slots, buckets)
    hit = arriving & (col == iota(shape, 1) // CAP) & (rank == iota(shape, 1) % CAP)
    pick = jnp.where(hit, 1.0, 0.0).astype(BF16)
    copies = []
    for t in range(steps):
        moved = dot_n(pick, outs[t])
        rows = pl.ds(t * slots, slots)
        conv_s[rows, :] = jnp.where(arriving, moved, conv_ref[t].astype(F32)).astype(BF16)
        copies.append(pltpu.make_async_copy(conv_s.at[rows], conv_out.at[rows], sems.at[t]))
        copies[t].start()
    lhs = conv_s[...]
    mix[...] = dot_t(lhs, proj_ref[0:width, :])
    rest = proj_ref.shape[0] - width
    low[:, 0:rest] = dot_t(lhs, proj_ref[width:, :])
    quarter = slots // 2 // SIDE
    for half, outs in ((0, (a0, a1, a2, a3)), (1, (b0, b1, b2, b3))):
        for d in range(SIDE):
            q = lax.rem(pos_ref[1 + half] + d, SIDE)
            out = outs[d]
            out[steps * quarter :, :] = jnp.zeros((8, width), F32)
            for t in range(steps):
                start = pl.multiple_of(t * slots + half * (slots // 2) + q * quarter, quarter)
                out[t * quarter : (t + 1) * quarter, :] = mix[pl.ds(start, quarter), :]
                for g in range(quarter // 8):
                    lane = 32 * (t * (quarter // 8) + g)
                    out[steps * quarter :, lane : lane + rest] = low[pl.ds(start + 8 * g, 8), 0:rest]
    for copy in copies:
        copy.wait()


def prepare(pos_ref, active_ref, pieces_x, pieces_y, conv_ref, dtw_ref, dtb_ref,
            step_ref, conv_out_ref, low_ref, rank_s, wait):
    total, width = conv_ref.shape
    slots = active_ref.shape[1]
    steps = total // slots
    quarter = slots // 2 // SIDE
    half = steps * quarter
    groups = quarter // 8
    rest = 32
    for axis, pieces in ((0, pieces_x), (1, pieces_y)):
        for d in range(SIDE):
            q = lax.rem(pos_ref[1 + axis] + (SIDE - d), SIDE)
            for t in range(steps):
                start = pl.multiple_of(t * slots + axis * (slots // 2) + q * quarter, quarter)
                rank_s[pl.ds(start, quarter), :] = pieces[d][t * quarter : (t + 1) * quarter, :].astype(BF16)
                for g in range(groups):
                    lane = 32 * (t * groups + g)
                    low_ref[pl.ds(start + 8 * g, 8), 0:rest] = pieces[d][half:, lane : lane + rest]
    alive = as_column(active_ref[...], slots) == 1
    wait()
    for t in range(steps):
        rows = slice(t * slots, (t + 1) * slots)
        conv_out_ref[rows, :] = conv_ref[rows, :].astype(F32)
        raw = dot_n(rank_s[rows, :], dtw_ref[...]) + dtb_ref[...]
        soft = jnp.maximum(raw, 0.0) + jnp.log1p(jnp.exp(-jnp.abs(raw)))
        step_ref[rows, :] = jnp.where(alive, soft, 0.0)


def stage_kernel(plan_ref, got_ref, state_ref, out_ref, spread_ref, sems):
    tiles, rows, _ = out_ref.shape
    buckets = sems.shape[1]
    states = got_ref.shape[0] // buckets
    parts = sems.shape[0]
    copies = []
    for l in range(tiles):
        for i in range(parts):
            here = pl.ds(i * (rows // parts), rows // parts)
            copies.append(
                pltpu.make_async_copy(state_ref.at[here, pl.ds(l * 128, 128)], out_ref.at[l, here], sems.at[i, l])
            )
    for copy in copies:
        copy.start()
    shape = spread_ref.shape
    spread_ref[...] = jnp.where(iota(shape, 0) % (shape[0] // 2) == iota(shape, 1) // 128, 1.0, 0.0).astype(BF16)
    for copy in copies:
        copy.wait()

    def patch(b, carry):
        gone = plan_ref[0, b]
        here = plan_ref[1, b]

        @pl.when(gone >= 0)
        def _():
            rows = pl.ds(pl.multiple_of(gone * states, states), states)
            for l in range(tiles):
                out_ref[l, rows, :] = jnp.zeros((states, 128), F32)

        @pl.when(here >= 0)
        def _():
            rows = pl.ds(pl.multiple_of(here * states, states), states)
            there = pl.ds(pl.multiple_of(b * states, states), states)
            for l in range(tiles):
                out_ref[l, rows, :] = got_ref[there, l * 128 : (l + 1) * 128]

        return carry

    lax.fori_loop(0, buckets, patch, 0)


PIECES = (64, 48, 16)


def scan_kernel(pos_ref, active_ref, x0, x1, x2, x3, y0, y1, y2, y3, state_s,
                spread_ref, conv_ref, gate_ref, dtw_ref, dtb_ref, rate_ref, gain_ref,
                gated_out, out_ref, alive_s, rate_s, final_s, step_s, conv_s, low_s, rank_s, gated_ref, wide_s,
                out_sems):
    steps, slots, width = gate_ref.shape
    states = rate_ref.shape[0]
    tiles = width // 128

    def stores(k):
        first = sum(PIECES[:k])
        slots_here = pl.ds(first, PIECES[k])
        rows = pl.ds(first * states, PIECES[k] * states)
        copies = [pltpu.make_async_copy(gated_ref.at[:, slots_here], gated_out.at[:, slots_here], out_sems.at[k, tiles])]
        for l in range(tiles):
            copies.append(
                pltpu.make_async_copy(final_s.at[l, rows], out_ref.at[rows, pl.ds(l * 128, 128)], out_sems.at[k, l])
            )
        return copies

    def ready():
        pass

    prepare(pos_ref, active_ref, (x0, x1, x2, x3), (y0, y1, y2, y3), conv_ref, dtw_ref, dtb_ref,
            step_s, conv_s, low_s, rank_s, ready)
    rest = 2 * states
    high = low_s[:, 0:rest].astype(BF16)
    rounding = (low_s[:, 0:rest] - high.astype(F32)).astype(BF16)
    wide_s[...] = dot_n(jnp.concatenate([high, rounding], axis=1), spread_ref[...])
    rate_s[...] = rate_ref[...] * (-1.0 / math.log(2.0))
    alive = as_column(active_ref[...], slots) == 1
    alive_s[...] = jnp.broadcast_to(jnp.where(alive, 1.0, 0.0), alive_s.shape)

    def group(base):
        dts, dxs, lows, accs = [], [], [], []
        for t in range(steps):
            rows = pl.ds(pl.multiple_of(t * slots + base, 8), 8)
            lows.append(rows)
            for l in range(tiles):
                lanes = slice(l * 128, (l + 1) * 128)
                dt = step_s[rows, lanes]
                cv = conv_s[rows, lanes]
                dts.append(dt)
                dxs.append(dt * cv)
                accs.append(gain_ref[:, lanes] * cv)
        for n in range(states):
            place = pl.ds(base * states + n, 8, stride=states)
            gives = [wide_s[rows, n * 128 : (n + 1) * 128] for rows in lows]
            takes = [wide_s[rows, (states + n) * 128 : (states + n + 1) * 128] for rows in lows]
            for l in range(tiles):
                st = state_s[l, place, :]
                rate = rate_s[n : n + 1, l * 128 : (l + 1) * 128]
                for t in range(steps):
                    k = t * tiles + l
                    st = jnp.exp2(dts[k] * rate) * st + dxs[k] * gives[t]
                    accs[k] = accs[k] + st * takes[t]
                final_s[l, place, :] = st
        return accs

    def pair(i, carry):
        base = pl.multiple_of(i * 16, 16)
        accs = [group(base), group(pl.multiple_of(base + 8, 8))]
        on = alive_s[pl.ds(base, 16), :] > 0.5
        for t in range(steps):
            for l in range(tiles):
                lanes = slice(l * 128, (l + 1) * 128)
                gate = jax.nn.silu(gate_ref[t, pl.ds(base, 16), lanes].astype(F32))
                value = jnp.concatenate([accs[0][t * tiles + l], accs[1][t * tiles + l]], axis=0) * gate
                gated_ref[t, pl.ds(base, 16), lanes] = jnp.where(on, value, 0.0).astype(BF16)
        return carry

    def block(i, carry):
        pair(i, carry)
        for k in range(len(PIECES)):

            @pl.when(i == sum(PIECES[: k + 1]) // 16 - 1)
            def _():
                for copy in stores(k):
                    copy.start()

        return carry

    lax.fori_loop(0, slots // 16, block, 0)
    for k in range(len(PIECES)):
        for copy in stores(k):
            copy.wait()


def in_hbm(value):
    return pltpu.with_memory_space_constraint(value, pltpu.HBM)


def on_device(projected, conv_weight, conv_bias, xproj_weight, dtproj_weight, dt_bias, a_rate, skip_gain,
              ssm_state, conv_cache, send_dest, recv_source, active):
    steps, slots, _, width = projected.shape
    rank_width = dtproj_weight.shape[0]
    states = a_rate.shape[0]
    taps = conv_weight.shape[0]
    peers = lax.axis_size("req")
    buckets = peers * CAP
    place = lax.axis_index("wa")
    pos = jnp.stack([lax.axis_index("req"), place // SIDE, place % SIDE]).astype(jnp.int32)
    send_row, recv_row, active_row = (in_hbm(v.reshape(1, slots)) for v in (send_dest, recv_source, active))
    recv_rows = recv_source.reshape(1, slots)
    bias, dt_row, gain = (v.reshape(1, width) for v in (conv_bias, dt_bias, skip_gain))
    cache = in_hbm(jnp.transpose(conv_cache, (1, 0, 2)))
    proj = jnp.transpose(xproj_weight, (1, 0))
    state_rows = in_hbm(ssm_state.reshape(slots * states, width))
    sds = jax.ShapeDtypeStruct

    compact = (taps - 1) * CAP * (width // 128)
    out_cache, plan = pl.pallas_call(
        pick_cache_kernel,
        out_shape=(sds((peers * compact, 128), F32), sds((2, slots), jnp.int32)),
        in_specs=[SM, HB, HB, HB],
        out_specs=(VM, VM),
        scratch_shapes=[
            pltpu.VMEM((1, slots), jnp.int32),
            pltpu.VMEM((1, slots), jnp.int32),
            pltpu.VMEM(cache.shape, BF16),
            pltpu.VMEM((peers * 8, width), F32),
            pltpu.SemaphoreType.DMA((3,)),
        ],
        compiler_params=pltpu.CompilerParams(vmem_limit_bytes=4 * MIB),
        name="pick_cache",
    )(pos, send_row, recv_row, cache)
    both = jnp.transpose(projected, (2, 0, 1, 3))
    got_cache = lax.all_to_all(
        out_cache.reshape(peers, compact, 128), "req", split_axis=0, concat_axis=0, tiled=True
    ).reshape(peers * compact, 128)

    out_state = pl.pallas_call(
        pick_state_kernel,
        out_shape=pltpu.HBM((buckets, states, width), F32),
        in_specs=[SM, HB],
        out_specs=HB,
        scratch_shapes=[
            pltpu.VMEM((buckets, states, width), F32),
            pltpu.SemaphoreType.DMA((buckets,)),
            pltpu.SemaphoreType.DMA((1,)),
        ],
        cost_estimate=pl.CostEstimate(flops=1, bytes_accessed=1, transcendentals=0),
        compiler_params=pltpu.CompilerParams(vmem_limit_bytes=4 * MIB),
        name="pick_state",
    )(plan, state_rows)

    total = steps * slots
    conv_main, gate, cache_out, x_arr = pl.pallas_call(
        conv_kernel,
        out_shape=(
            sds((steps, slots, width), BF16),
            pltpu.HBM((steps, slots, width), BF16),
            sds((taps - 1, slots, width), BF16),
            sds((steps * buckets, width), BF16),
        ),
        in_specs=[SM] + [HB] * 3 + [VM] + [HB] * 3,
        out_specs=(VM, HB, VM, VM),
        scratch_shapes=[
            pltpu.SemaphoreType.DMA((1,)),
            pltpu.VMEM((1, slots), jnp.int32),
            pltpu.VMEM((1, slots), jnp.int32),
            pltpu.VMEM((1, slots), jnp.int32),
            pltpu.VMEM(cache.shape, BF16),
            pltpu.VMEM(conv_weight.shape, BF16),
            pltpu.VMEM((1, width), F32),
            pltpu.SemaphoreType.DMA((6,)),
        ],
        compiler_params=pltpu.CompilerParams(vmem_limit_bytes=8 * MIB),
        name="convolve",
    )(pos, send_row, recv_row, active_row, both, cache, in_hbm(conv_weight), in_hbm(bias))

    out_state, conv_main, x_arr = lax.optimization_barrier((out_state, conv_main, x_arr))
    half = steps * (slots // 2 // SIDE)
    projected_parts = pl.pallas_call(
        project_kernel,
        out_shape=(pltpu.HBM((total, width), BF16),) + (sds((half + 8, width), F32),) * (2 * SIDE),
        in_specs=[SM] + [VM] * 7,
        out_specs=(HB,) + (VM,) * (2 * SIDE),
        scratch_shapes=[
            pltpu.VMEM((total, width), F32),
            pltpu.VMEM((total, 128), F32),
            pltpu.VMEM((peers * 8, width), F32),
            pltpu.VMEM((total, width), BF16),
            pltpu.SemaphoreType.DMA((3,)),
        ],
        compiler_params=pltpu.CompilerParams(vmem_limit_bytes=8 * MIB),
        name="project",
    )(pos, recv_rows, got_cache, x_arr, conv_main, conv_weight, bias, proj)
    conv_all = projected_parts[0]
    own_a, own_b = projected_parts[1 : 1 + SIDE], projected_parts[1 + SIDE :]

    def gathered(value, axis, parts):
        return [value] + [lax.ppermute(parts[d - 1], "wa", shift(axis, d)) for d in range(1, SIDE)]

    def summed(value, axis, parts):
        pieces = gathered(value, axis, parts)
        return pieces[0] + pieces[1] + pieces[2] + pieces[3]

    sum_a = summed(own_a[0], 0, own_a[1:])
    sum_b = summed(own_b[0], 1, own_b[1:])
    got_state = lax.all_to_all(out_state, "req", split_axis=0, concat_axis=0, tiled=True)
    all_a = summed(sum_a, 1, [sum_a] * 3)
    all_b = summed(sum_b, 0, [sum_b] * 3)
    last_x = gathered(all_a, 0, [all_a] * 3)
    last_y = gathered(all_b, 1, [all_b] * 3)

    tiles = width // 128
    staged, spread = pl.pallas_call(
        stage_kernel,
        out_shape=(sds((tiles, slots * states, 128), F32), sds((4 * states, 2 * states * 128), BF16)),
        in_specs=[SM, VM, HB],
        out_specs=(VM, VM),
        scratch_shapes=[pltpu.SemaphoreType.DMA((1, buckets))],
        compiler_params=pltpu.CompilerParams(vmem_limit_bytes=8 * MIB),
        cost_estimate=pl.CostEstimate(flops=0, bytes_accessed=12 * MIB, transcendentals=0),
        name="stage_state",
    )(plan, got_state.reshape(buckets * states, width), state_rows)

    gated_out, state_out = pl.pallas_call(
        scan_kernel,
        out_shape=(sds((steps, slots, width), BF16), sds((slots * states, width), F32)),
        in_specs=[SM] + [VM] * 17,
        out_specs=(HB, HB),
        scratch_shapes=[
            pltpu.VMEM((slots, 128), F32),
            pltpu.VMEM((states, width), F32),
            pltpu.VMEM((tiles, slots * states, 128), F32),
            pltpu.VMEM((total, width), F32),
            pltpu.VMEM((total, width), F32),
            pltpu.VMEM((total, 128), F32),
            pltpu.VMEM((total, width), BF16),
            pltpu.VMEM((steps, slots, width), BF16),
            pltpu.VMEM((total, 2 * states * 128), F32),
            pltpu.SemaphoreType.DMA((len(PIECES), tiles + 1)),
        ],
        compiler_params=pltpu.CompilerParams(vmem_limit_bytes=20 * MIB),
        name="scan",
    )(
        pos, active.reshape(1, slots), *last_x, *last_y, staged, spread, conv_all, gate, dtproj_weight, dt_row,
        a_rate, gain,
    )
    return (
        gated_out,
        state_out.reshape(slots, states, width),
        jnp.transpose(cache_out, (1, 0, 2)),
    )


def solution(mesh):
    return jax.shard_map(
        on_device,
        mesh=mesh,
        in_specs=(
            P(None, "req", None, "wa"),
            P(None, "wa"),
            P("wa"),
            P("wa", None),
            P(None, "wa"),
            P("wa"),
            P(None, "wa"),
            P("wa"),
            P("req", None, "wa"),
            P("req", None, "wa"),
            P("req"),
            P("req"),
            P("req"),
        ),
        out_specs=(P(None, "req", "wa"), P("req", None, "wa"), P("req", None, "wa")),
        check_vma=False,
    )
```

```python
import math

import jax
import jax.numpy as jnp
from jax import lax
from jax.experimental import pallas as pl
from jax.experimental.pallas import tpu as pltpu
from jax.sharding import PartitionSpec as P

CAP = 2
SIDE = 4
MIB = 1 << 20
F32 = jnp.float32
BF16 = jnp.bfloat16
VM = pl.BlockSpec(memory_space=pltpu.VMEM)
SM = pl.BlockSpec(memory_space=pltpu.SMEM)
HB = pl.BlockSpec(memory_space=pltpu.HBM)


def shift(axis, amount):
    pairs = []
    for x in range(SIDE):
        for y in range(SIDE):
            tx, ty = (x + amount) % SIDE, y
            if axis == 1:
                tx, ty = x, (y + amount) % SIDE
            pairs.append((x * SIDE + y, tx * SIDE + ty))
    return pairs


def dot_t(lhs, rhs):
    return lax.dot_general(lhs, rhs, (((1,), (1,)), ((), ())), preferred_element_type=F32)


def dot_n(lhs, rhs):
    return jnp.dot(lhs, rhs, preferred_element_type=F32)


def iota(shape, dim):
    return lax.broadcasted_iota(jnp.int32, shape, dim)


def as_column(row, size):
    eye = iota((size, size), 0) == iota((size, size), 1)
    return jnp.sum(jnp.where(eye, jnp.broadcast_to(row, (size, size)), 0), axis=1, keepdims=True)


def ranks_row(row, col, size):
    earlier = (col == row) & (iota((size, size), 0) < iota((size, size), 1))
    return jnp.sum(jnp.where(earlier, 1, 0), axis=0, keepdims=True)


def ranks_col(row, col, size):
    earlier = (col == row) & (iota((size, size), 1) < iota((size, size), 0))
    return jnp.sum(jnp.where(earlier, 1, 0), axis=1, keepdims=True)


def fetch(pairs, sems):
    copies = [pltpu.make_async_copy(a, b, sems.at[i]) for i, (a, b) in enumerate(pairs)]
    for copy in copies:
        copy.start()
    return copies


def pick_cache_kernel(pos_ref, dest_hbm, source_hbm, cache_hbm, out_ref, plan_ref, dest_ref, source_ref, cache_ref,
                      full_s, sems):
    copies = fetch(((dest_hbm, dest_ref), (source_hbm, source_ref), (cache_hbm, cache_ref)), sems)
    for copy in copies[:2]:
        copy.wait()
    taps, slots, _ = cache_ref.shape
    own = pos_ref[0]
    row = dest_ref[...]
    col = as_column(row, slots)
    rank = ranks_row(row, col, slots)
    rows = full_s.shape[0]
    shape = (rows, slots)
    target = iota(shape, 0) // 8
    place = iota(shape, 0) % 8
    total = jnp.zeros(full_s.shape, F32)
    square = (slots, slots)
    bucket = iota(square, 1)
    for k, ref in enumerate((dest_ref, source_ref)):
        plan_row = ref[...]
        plan_col = as_column(plan_row, slots)
        hit = (plan_col != own) & (plan_col == bucket // CAP) & (ranks_col(plan_row, plan_col, slots) == bucket % CAP)
        plan_ref[k : k + 1, :] = jnp.sum(jnp.where(hit, iota(square, 0) + 1, 0), axis=0, keepdims=True) - 1
    copies[2].wait()
    hit = (row == target) & (row != own) & (rank == place % CAP)
    for tap in range(taps):
        pick = jnp.where(hit & (place // CAP == tap), 1.0, 0.0).astype(BF16)
        total = total + dot_n(pick, cache_ref[tap])
    full_s[...] = total
    used = taps * CAP
    tiles = full_s.shape[1] // 128
    for d in range(rows // 8):
        for l in range(tiles):
            start = (d * tiles + l) * used
            out_ref[start : start + used, :] = full_s[8 * d : 8 * d + used, l * 128 : (l + 1) * 128]


def pick_state_kernel(plan_ref, state_ref, out_hbm, out_ref, sems, out_sem):
    buckets, states, _ = out_ref.shape
    copies = []
    for b in range(buckets):
        rows = pl.ds(pl.multiple_of(jnp.maximum(plan_ref[0, b], 0) * states, states), states)
        copies.append(pltpu.make_async_copy(state_ref.at[rows], out_ref.at[b], sems.at[b]))
    for copy in copies:
        copy.start()
    for copy in copies:
        copy.wait()
    copy = pltpu.make_async_copy(out_ref, out_hbm, out_sem.at[0])
    copy.start()
    copy.wait()


def conv_steps(window, taps_ref, bias, steps):
    taps = taps_ref[...].astype(F32)
    outs = []
    for t in range(steps):
        total = bias
        for k in range(taps.shape[0]):
            total = total + taps[k : k + 1, :] * window[t + k]
        outs.append(jax.nn.silu(total).astype(BF16))
    return outs


def conv_kernel(pos_ref, dest_hbm, source_hbm, active_hbm, both_ref, cache_hbm, taps_hbm, bias_hbm,
                conv_ref, gate_out, cache_out_ref, arr_ref, sems,
                dest_ref, source_ref, active_ref, cache_ref, taps_ref, bias_ref, in_sems):
    x_ref = both_ref.at[0]
    copies = fetch(
        ((dest_hbm, dest_ref), (source_hbm, source_ref), (active_hbm, active_ref), (cache_hbm, cache_ref),
         (taps_hbm, taps_ref), (bias_hbm, bias_ref)),
        in_sems,
    )
    gate_copy = pltpu.make_async_copy(both_ref.at[1], gate_out, sems.at[0])
    gate_copy.start()
    for copy in copies:
        copy.wait()
    steps, slots, width = x_ref.shape
    taps = cache_ref.shape[0]
    own = pos_ref[0]
    dest = as_column(dest_ref[...], slots)
    alive = as_column(active_ref[...], slots)
    step = 16
    for r in range(0, slots, step):
        rows = slice(r, r + step)
        keep = [cache_ref[j, rows, :] for j in range(taps)]
        new = [x_ref[t, rows, :] for t in range(steps)]
        outs = conv_steps([v.astype(F32) for v in keep + new], taps_ref, bias_ref[...], steps)
        for t in range(steps):
            conv_ref[t, rows, :] = outs[t]
        on = alive[rows, :] == 1
        gone = dest[rows, :] != own
        for j in range(taps):
            old = jnp.where(gone, 0.0, keep[j].astype(F32))
            cache_out_ref[j, rows, :] = jnp.where(on, new[j].astype(F32), old).astype(BF16)
    buckets = arr_ref.shape[0] // steps
    row = source_ref[...]
    rank = ranks_row(row, as_column(row, slots), slots)
    shape = (buckets, slots)
    hit = (row == iota(shape, 0) // CAP) & (row != own) & (rank == iota(shape, 0) % CAP)
    pick = jnp.where(hit, 1.0, 0.0).astype(BF16)
    for t in range(steps):
        arr_ref[t * buckets : (t + 1) * buckets, :] = dot_n(pick, x_ref[t]).astype(BF16)
    gate_copy.wait()


def project_kernel(pos_ref, source_ref, got_ref, arr_ref, conv_ref, taps_ref, bias_ref, proj_ref,
                   conv_out, a0, a1, a2, a3, b0, b1, b2, b3, mix, low, full_s, conv_s, sems):
    steps, slots, width = conv_ref.shape
    buckets = arr_ref.shape[0] // steps
    used = (taps_ref.shape[0] - 1) * CAP
    tiles = width // 128
    full_s[...] = jnp.zeros(full_s.shape, F32)
    for d in range(full_s.shape[0] // 8):
        for l in range(tiles):
            start = (d * tiles + l) * used
            full_s[8 * d : 8 * d + used, l * 128 : (l + 1) * 128] = got_ref[start : start + used, :]
    got = full_s[...].astype(BF16)
    shape = (buckets, got.shape[0])
    window = []
    for j in range(taps_ref.shape[0] - 1):
        place = (iota(shape, 0) // CAP) * 8 + j * CAP + iota(shape, 0) % CAP
        window.append(dot_n(jnp.where(iota(shape, 1) == place, 1.0, 0.0).astype(BF16), got))
    for t in range(steps):
        window.append(arr_ref[t * buckets : (t + 1) * buckets, :].astype(F32))
    outs = conv_steps(window, taps_ref, bias_ref[...], steps)
    row = source_ref[...]
    col = as_column(row, slots)
    rank = ranks_col(row, col, slots)
    arriving = col != pos_ref[0]
    shape = (slots, buckets)
    hit = arriving & (col == iota(shape, 1) // CAP) & (rank == iota(shape, 1) % CAP)
    pick = jnp.where(hit, 1.0, 0.0).astype(BF16)
    copies = []
    for t in range(steps):
        moved = dot_n(pick, outs[t])
        rows = pl.ds(t * slots, slots)
        conv_s[rows, :] = jnp.where(arriving, moved, conv_ref[t].astype(F32)).astype(BF16)
        copies.append(pltpu.make_async_copy(conv_s.at[rows], conv_out.at[rows], sems.at[t]))
        copies[t].start()
    lhs = conv_s[...]
    mix[...] = dot_t(lhs, proj_ref[0:width, :])
    rest = proj_ref.shape[0] - width
    low[:, 0:rest] = dot_t(lhs, proj_ref[width:, :])
    quarter = slots // 2 // SIDE
    for half, outs in ((0, (a0, a1, a2, a3)), (1, (b0, b1, b2, b3))):
        for d in range(SIDE):
            q = lax.rem(pos_ref[1 + half] + d, SIDE)
            out = outs[d]
            out[steps * quarter :, :] = jnp.zeros((8, width), F32)
            for t in range(steps):
                start = pl.multiple_of(t * slots + half * (slots // 2) + q * quarter, quarter)
                out[t * quarter : (t + 1) * quarter, :] = mix[pl.ds(start, quarter), :]
                for g in range(quarter // 8):
                    lane = 32 * (t * (quarter // 8) + g)
                    out[steps * quarter :, lane : lane + rest] = low[pl.ds(start + 8 * g, 8), 0:rest]
    for copy in copies:
        copy.wait()


def prepare(pos_ref, active_ref, pieces_x, pieces_y, conv_ref, dtw_ref, dtb_ref,
            step_ref, conv_out_ref, low_ref, rank_s, wait):
    total, width = conv_ref.shape
    slots = active_ref.shape[1]
    steps = total // slots
    quarter = slots // 2 // SIDE
    half = steps * quarter
    groups = quarter // 8
    rest = 32
    for axis, pieces in ((0, pieces_x), (1, pieces_y)):
        for d in range(SIDE):
            q = lax.rem(pos_ref[1 + axis] + (SIDE - d), SIDE)
            for t in range(steps):
                start = pl.multiple_of(t * slots + axis * (slots // 2) + q * quarter, quarter)
                rank_s[pl.ds(start, quarter), :] = pieces[d][t * quarter : (t + 1) * quarter, :].astype(BF16)
                for g in range(groups):
                    lane = 32 * (t * groups + g)
                    low_ref[pl.ds(start + 8 * g, 8), 0:rest] = pieces[d][half:, lane : lane + rest]
    alive = as_column(active_ref[...], slots) == 1
    wait()
    for t in range(steps):
        rows = slice(t * slots, (t + 1) * slots)
        conv_out_ref[rows, :] = conv_ref[rows, :].astype(F32)
        raw = dot_n(rank_s[rows, :], dtw_ref[...]) + dtb_ref[...]
        soft = jnp.maximum(raw, 0.0) + jnp.log1p(jnp.exp(-jnp.abs(raw)))
        step_ref[rows, :] = jnp.where(alive, soft, 0.0)


PITCH = 24


def stage_kernel(plan_ref, got_ref, state_ref, out_ref, spread_ref, sems):
    tiles = out_ref.shape[0]
    buckets = sems.shape[0]
    states = state_ref.shape[1]
    copies = []
    for l in range(tiles):
        lanes = pl.ds(l * 128, 128)
        copies.append(
            pltpu.make_async_copy(state_ref.at[:, :, lanes], out_ref.at[l, :, pl.ds(0, states), :], sems.at[l])
        )
    for copy in copies:
        copy.start()
    shape = spread_ref.shape
    spread_ref[...] = jnp.where(iota(shape, 0) % (shape[0] // 2) == iota(shape, 1) // 128, 1.0, 0.0).astype(BF16)
    for copy in copies:
        copy.wait()

    def patch(b, carry):
        gone = plan_ref[0, b]
        here = plan_ref[1, b]

        @pl.when(gone >= 0)
        def _():
            for l in range(tiles):
                out_ref[l, gone, 0:states, :] = jnp.zeros((states, 128), F32)

        @pl.when(here >= 0)
        def _():
            there = pl.ds(pl.multiple_of(b * states, states), states)
            for l in range(tiles):
                out_ref[l, here, 0:states, :] = got_ref[there, l * 128 : (l + 1) * 128]

        return carry

    lax.fori_loop(0, buckets, patch, 0)


PIECES = (48, 32, 16, 16, 16)


def scan_kernel(pos_ref, active_ref, x0, x1, x2, x3, y0, y1, y2, y3, state_s,
                spread_ref, conv_ref, gate_ref, dtw_ref, dtb_ref, rate_ref, gain_ref,
                gated_out, out_ref, alive_s, rate_s, final_s, step_s, conv_s, low_s, rank_s, gated_ref, wide_s,
                out_sems):
    steps, slots, width = gate_ref.shape
    states = rate_ref.shape[0]
    tiles = width // 128

    def stores(k):
        first = sum(PIECES[:k])
        slots_here = pl.ds(first, PIECES[k])
        copies = [pltpu.make_async_copy(gated_ref.at[:, slots_here], gated_out.at[:, slots_here], out_sems.at[k, tiles])]
        for l in range(tiles):
            copies.append(
                pltpu.make_async_copy(
                    final_s.reshape(tiles, slots, PITCH, 128).at[l, slots_here, pl.ds(0, states), :],
                    out_ref.at[slots_here, :, pl.ds(l * 128, 128)],
                    out_sems.at[k, l],
                )
            )
        return copies

    def ready():
        pass

    prepare(pos_ref, active_ref, (x0, x1, x2, x3), (y0, y1, y2, y3), conv_ref, dtw_ref, dtb_ref,
            step_s, conv_s, low_s, rank_s, ready)
    rest = 2 * states
    high = low_s[:, 0:rest].astype(BF16)
    rounding = (low_s[:, 0:rest] - high.astype(F32)).astype(BF16)
    wide_s[...] = dot_n(jnp.concatenate([high, rounding], axis=1), spread_ref[...])
    rate_s[...] = rate_ref[...] * (-1.0 / math.log(2.0))
    alive = as_column(active_ref[...], slots) == 1
    alive_s[...] = jnp.broadcast_to(jnp.where(alive, 1.0, 0.0), alive_s.shape)

    def group(base):
        dts, dxs, lows, accs = [], [], [], []
        for t in range(steps):
            rows = pl.ds(pl.multiple_of(t * slots + base, 8), 8)
            lows.append(rows)
            for l in range(tiles):
                lanes = slice(l * 128, (l + 1) * 128)
                dt = step_s[rows, lanes]
                cv = conv_s[rows, lanes]
                dts.append(dt)
                dxs.append(dt * cv)
                accs.append(gain_ref[:, lanes] * cv)
        for n in range(states):
            place = pl.ds(base * PITCH + n, 8, stride=PITCH)
            gives = [wide_s[rows, n * 128 : (n + 1) * 128] for rows in lows]
            takes = [wide_s[rows, (states + n) * 128 : (states + n + 1) * 128] for rows in lows]
            for l in range(tiles):
                st = state_s[l, place, :]
                rate = rate_s[n : n + 1, l * 128 : (l + 1) * 128]
                for t in range(steps):
                    k = t * tiles + l
                    st = jnp.exp2(dts[k] * rate) * st + dxs[k] * gives[t]
                    accs[k] = accs[k] + st * takes[t]
                final_s[l, place, :] = st
        return accs

    def pair(i, carry):
        base = pl.multiple_of(i * 16, 16)
        accs = [group(base), group(pl.multiple_of(base + 8, 8))]
        on = alive_s[pl.ds(base, 16), :] > 0.5
        for t in range(steps):
            for l in range(tiles):
                lanes = slice(l * 128, (l + 1) * 128)
                gate = jax.nn.silu(gate_ref[t, pl.ds(base, 16), lanes].astype(F32))
                value = jnp.concatenate([accs[0][t * tiles + l], accs[1][t * tiles + l]], axis=0) * gate
                gated_ref[t, pl.ds(base, 16), lanes] = jnp.where(on, value, 0.0).astype(BF16)
        return carry

    def block(i, carry):
        pair(i, carry)
        for k in range(len(PIECES)):

            @pl.when(i == sum(PIECES[: k + 1]) // 16 - 1)
            def _():
                for copy in stores(k):
                    copy.start()

        return carry

    lax.fori_loop(0, slots // 16, block, 0)
    for k in range(len(PIECES)):
        for copy in stores(k):
            copy.wait()


def in_hbm(value):
    return pltpu.with_memory_space_constraint(value, pltpu.HBM)


def on_device(projected, conv_weight, conv_bias, xproj_weight, dtproj_weight, dt_bias, a_rate, skip_gain,
              ssm_state, conv_cache, send_dest, recv_source, active):
    steps, slots, _, width = projected.shape
    rank_width = dtproj_weight.shape[0]
    states = a_rate.shape[0]
    taps = conv_weight.shape[0]
    peers = lax.axis_size("req")
    buckets = peers * CAP
    place = lax.axis_index("wa")
    pos = jnp.stack([lax.axis_index("req"), place // SIDE, place % SIDE]).astype(jnp.int32)
    send_row, recv_row, active_row = (in_hbm(v.reshape(1, slots)) for v in (send_dest, recv_source, active))
    recv_rows = recv_source.reshape(1, slots)
    bias, dt_row, gain = (v.reshape(1, width) for v in (conv_bias, dt_bias, skip_gain))
    cache = in_hbm(jnp.transpose(conv_cache, (1, 0, 2)))
    proj = jnp.transpose(xproj_weight, (1, 0))
    state_rows = in_hbm(ssm_state.reshape(slots * states, width))
    sds = jax.ShapeDtypeStruct

    compact = (taps - 1) * CAP * (width // 128)
    out_cache, plan = pl.pallas_call(
        pick_cache_kernel,
        out_shape=(sds((peers * compact, 128), F32), sds((2, slots), jnp.int32)),
        in_specs=[SM, HB, HB, HB],
        out_specs=(VM, VM),
        scratch_shapes=[
            pltpu.VMEM((1, slots), jnp.int32),
            pltpu.VMEM((1, slots), jnp.int32),
            pltpu.VMEM(cache.shape, BF16),
            pltpu.VMEM((peers * 8, width), F32),
            pltpu.SemaphoreType.DMA((3,)),
        ],
        compiler_params=pltpu.CompilerParams(vmem_limit_bytes=4 * MIB),
        name="pick_cache",
    )(pos, send_row, recv_row, cache)
    both = jnp.transpose(projected, (2, 0, 1, 3))
    got_cache = lax.all_to_all(
        out_cache.reshape(peers, compact, 128), "req", split_axis=0, concat_axis=0, tiled=True
    ).reshape(peers * compact, 128)

    out_state = pl.pallas_call(
        pick_state_kernel,
        out_shape=pltpu.HBM((buckets, states, width), F32),
        in_specs=[SM, HB],
        out_specs=HB,
        scratch_shapes=[
            pltpu.VMEM((buckets, states, width), F32),
            pltpu.SemaphoreType.DMA((buckets,)),
            pltpu.SemaphoreType.DMA((1,)),
        ],
        cost_estimate=pl.CostEstimate(flops=1, bytes_accessed=1, transcendentals=0),
        compiler_params=pltpu.CompilerParams(vmem_limit_bytes=4 * MIB),
        name="pick_state",
    )(plan, state_rows)

    total = steps * slots
    conv_main, gate, cache_out, x_arr = pl.pallas_call(
        conv_kernel,
        out_shape=(
            sds((steps, slots, width), BF16),
            pltpu.HBM((steps, slots, width), BF16),
            sds((taps - 1, slots, width), BF16),
            sds((steps * buckets, width), BF16),
        ),
        in_specs=[SM] + [HB] * 3 + [VM] + [HB] * 3,
        out_specs=(VM, HB, VM, VM),
        scratch_shapes=[
            pltpu.SemaphoreType.DMA((1,)),
            pltpu.VMEM((1, slots), jnp.int32),
            pltpu.VMEM((1, slots), jnp.int32),
            pltpu.VMEM((1, slots), jnp.int32),
            pltpu.VMEM(cache.shape, BF16),
            pltpu.VMEM(conv_weight.shape, BF16),
            pltpu.VMEM((1, width), F32),
            pltpu.SemaphoreType.DMA((6,)),
        ],
        compiler_params=pltpu.CompilerParams(vmem_limit_bytes=8 * MIB),
        name="convolve",
    )(pos, send_row, recv_row, active_row, both, cache, in_hbm(conv_weight), in_hbm(bias))

    out_state, conv_main, x_arr = lax.optimization_barrier((out_state, conv_main, x_arr))
    half = steps * (slots // 2 // SIDE)
    projected_parts = pl.pallas_call(
        project_kernel,
        out_shape=(pltpu.HBM((total, width), BF16),) + (sds((half + 8, width), F32),) * (2 * SIDE),
        in_specs=[SM] + [VM] * 7,
        out_specs=(HB,) + (VM,) * (2 * SIDE),
        scratch_shapes=[
            pltpu.VMEM((total, width), F32),
            pltpu.VMEM((total, 128), F32),
            pltpu.VMEM((peers * 8, width), F32),
            pltpu.VMEM((total, width), BF16),
            pltpu.SemaphoreType.DMA((3,)),
        ],
        compiler_params=pltpu.CompilerParams(vmem_limit_bytes=8 * MIB),
        name="project",
    )(pos, recv_rows, got_cache, x_arr, conv_main, conv_weight, bias, proj)
    conv_all = projected_parts[0]
    own_a, own_b = projected_parts[1 : 1 + SIDE], projected_parts[1 + SIDE :]

    def gathered(value, axis, parts):
        return [value] + [lax.ppermute(parts[d - 1], "wa", shift(axis, d)) for d in range(1, SIDE)]

    def summed(value, axis, parts):
        pieces = gathered(value, axis, parts)
        return pieces[0] + pieces[1] + pieces[2] + pieces[3]

    sum_a = summed(own_a[0], 0, own_a[1:])
    sum_b = summed(own_b[0], 1, own_b[1:])
    got_state = lax.all_to_all(out_state, "req", split_axis=0, concat_axis=0, tiled=True)
    all_a = summed(sum_a, 1, [sum_a] * 3)
    all_b = summed(sum_b, 0, [sum_b] * 3)
    last_x = gathered(all_a, 0, [all_a] * 3)
    last_y = gathered(all_b, 1, [all_b] * 3)

    tiles = width // 128
    staged, spread = pl.pallas_call(
        stage_kernel,
        out_shape=(sds((tiles, slots, PITCH, 128), F32), sds((4 * states, 2 * states * 128), BF16)),
        in_specs=[SM, VM, HB],
        out_specs=(VM, VM),
        scratch_shapes=[pltpu.SemaphoreType.DMA((buckets,))],
        compiler_params=pltpu.CompilerParams(vmem_limit_bytes=8 * MIB),
        cost_estimate=pl.CostEstimate(flops=0, bytes_accessed=12 * MIB, transcendentals=0),
        name="stage_state",
    )(plan, got_state.reshape(buckets * states, width), in_hbm(ssm_state))

    gated_out, state_out = pl.pallas_call(
        scan_kernel,
        out_shape=(sds((steps, slots, width), BF16), sds((slots, states, width), F32)),
        in_specs=[SM] + [VM] * 17,
        out_specs=(HB, HB),
        scratch_shapes=[
            pltpu.VMEM((slots, 128), F32),
            pltpu.VMEM((states, width), F32),
            pltpu.VMEM((tiles, slots * PITCH, 128), F32),
            pltpu.VMEM((total, width), F32),
            pltpu.VMEM((total, width), F32),
            pltpu.VMEM((total, 128), F32),
            pltpu.VMEM((total, width), BF16),
            pltpu.VMEM((steps, slots, width), BF16),
            pltpu.VMEM((total, 2 * states * 128), F32),
            pltpu.SemaphoreType.DMA((len(PIECES), tiles + 1)),
        ],
        compiler_params=pltpu.CompilerParams(vmem_limit_bytes=24 * MIB),
        name="scan",
    )(
        pos, active.reshape(1, slots), *last_x, *last_y, staged.reshape(tiles, slots * PITCH, 128), spread, conv_all, gate, dtproj_weight, dt_row,
        a_rate, gain,
    )
    return (
        gated_out,
        state_out,
        jnp.transpose(cache_out, (1, 0, 2)),
    )


def solution(mesh):
    return jax.shard_map(
        on_device,
        mesh=mesh,
        in_specs=(
            P(None, "req", None, "wa"),
            P(None, "wa"),
            P("wa"),
            P("wa", None),
            P(None, "wa"),
            P("wa"),
            P(None, "wa"),
            P("wa"),
            P("req", None, "wa"),
            P("req", None, "wa"),
            P("req"),
            P("req"),
            P("req"),
        ),
        out_specs=(P(None, "req", "wa"), P("req", None, "wa"), P("req", None, "wa")),
        check_vma=False,
    )
```
